768 devices in a mesh: gx: 12 (over z), gy: 4 (over x_lo, core), gz: 16 (over x_hi, y).
Axes of the slice: x: 4 (x_hi: 2, x_lo: 2; x = x_hi * 2 + x_lo), y: 8, z: 12, core: 2. Of those that a mesh axis runs over, the one named last changes fastest.
Arguments:
- flow_pops: float32 [19, 48, 32, 2048], P(None, 'gx', 'gy', 'gz'), may hold values from 0.3 to 0.8
- phase_pops: float32 [7, 48, 32, 2048], P(None, 'gx', 'gy', 'gz'), may hold values from -0.15 to 0.15
- pore_mask: int32 [48, 32, 2048], P('gx', 'gy', 'gz'), may hold values from 0 to 1, as said below
Outputs:
- flow_next: float32 [19, 48, 32, 2048], P(None, 'gx', 'gy', 'gz')
- phase_next: float32 [7, 48, 32, 2048], P(None, 'gx', 'gy', 'gz')
The draws below stay inside these ranges and needn't reach their ends.
Inputs may be any that keep to these rules, and one draw needn't show every extreme that they name: `pore_mask`: 1 marks a pore voxel, 0 a rock voxel. Pores and rock form clusters several voxels wide, and whole aligned blocks of 4 x 8 x 128 voxels may be rock.
All inputs are finite; a program needn't handle non-finite values.
Results may differ from the reference program's by a relative error of at most 0.0003.
Values sent between devices are 32-bit elements; how exact they have to be, the bound alone decides.
A program may use at most 32 MiB of HBM per device.

```python
import jax
import jax.numpy as jnp
from jax import lax

CX = 4
CY = 8
CZ = 128
STEPS = 2
QF = 19
QG = 7
NX = 48
NY = 32
NZ = 2048


def draw_pore_mask(key, part):
    key_block = jax.random.fold_in(key, 11)
    key_cell = jax.random.fold_in(key, 23)
    blocks = jax.random.randint(key_block, (NX // CX, NY // CY, NZ // CZ), 0, 10)
    keep = (blocks >= 2).astype(jnp.int32)
    keep_full = jnp.repeat(jnp.repeat(jnp.repeat(keep, CX, axis=0), CY, axis=1), CZ, axis=2)
    noise = jax.random.randint(key_cell, (NX, NY, NZ), 0, 16)
    total = jnp.zeros((NX, NY, NZ), jnp.int32)
    for shift_x in (-1, 0, 1):
        for shift_y in (-1, 0, 1):
            for shift_z in (-1, 0, 1):
                total = total + jnp.roll(noise, (shift_x, shift_y, shift_z), axis=(0, 1, 2))
    pore = (total >= 190).astype(jnp.int32)
    return pore * keep_full


def block_scale(key, shape, split, smallest, top_value):
    loudness = 1.0
    for position, shards_of in split:
        steps = jax.random.uniform(jax.random.fold_in(jax.random.fold_in(key, 6), position), (shards_of,), jnp.float32, smallest / len(split), top_value / len(split))
        loudness = loudness * jnp.repeat(jnp.exp(steps), shape[position] // shards_of).reshape((-1,) + (1,) * (len(shape) - 1 - position))
    return loudness


def setup_inputs(seed: int = 0) -> dict:
    seeds = jax.random.split(jax.random.key(seed), 4)
    return {
        "flow_pops": jnp.clip(0.3 + 0.5 * jax.random.uniform(seeds[0], (QF, NX, NY, NZ), jnp.float32) ** block_scale(seeds[0], (QF, NX, NY, NZ), ((1, 12), (2, 4), (3, 16)), -0.2, 0.2), 0.3, 0.8),
        "phase_pops": jnp.clip(jax.random.uniform(seeds[1], (QG, NX, NY, NZ), jnp.float32, -0.15, 0.15) * block_scale(seeds[1], (QG, NX, NY, NZ), ((1, 12), (2, 4), (3, 16)), -0.4, 0.0), -0.15, 0.15),
        "pore_mask": draw_pore_mask(jax.random.fold_in(seeds[3], 71), 0),
    }


VEL_F = [(0, 0, 0), (1, 0, 0), (-1, 0, 0), (0, 1, 0), (0, -1, 0), (0, 0, 1), (0, 0, -1), (1, 1, 0), (-1, -1, 0), (1, -1, 0), (-1, 1, 0), (1, 0, 1), (-1, 0, -1), (1, 0, -1), (-1, 0, 1), (0, 1, 1), (0, -1, -1), (0, 1, -1), (0, -1, 1)]
OPP_F = [0, 2, 1, 4, 3, 6, 5, 8, 7, 10, 9, 12, 11, 14, 13, 16, 15, 18, 17]
WT_F = [1.0 / 3.0] + [1.0 / 18.0] * 6 + [1.0 / 36.0] * 12
BT_F = [-2.0 / 9.0] + [1.0 / 54.0] * 6 + [1.0 / 27.0] * 12
WT_G = [0.25] + [0.125] * 6
VEL_ALL = VEL_F + VEL_F[:7]
OPP_ALL = OPP_F + [19 + other for other in OPP_F[:7]]

def relax(flow_pops, phase_pops, phase, grads, fluid):
    density = sum((flow_pops[member] for member in range(19)))
    flow = [sum((VEL_F[member][dim] * flow_pops[member] for member in range(19))) / density for dim in range(3)]
    speed_sq = flow[0] * flow[0] + flow[1] * flow[1] + flow[2] * flow[2]
    omega = 1.0 / (0.8 + 0.2 * phase)
    grad_mag = jnp.sqrt(grads[0] * grads[0] + grads[1] * grads[1] + grads[2] * grads[2] + 0.01)
    results = []
    for member in range(19):
        offset = VEL_F[member]
        along = offset[0] * flow[0] + offset[1] * flow[1] + offset[2] * flow[2]
        cross = offset[0] * grads[0] + offset[1] * grads[1] + offset[2] * grads[2]
        balance = WT_F[member] * density * (1.0 + 3.0 * along + 4.5 * along * along - 1.5 * speed_sq)
        perturb = 0.5 * (WT_F[member] * cross * cross / grad_mag - BT_F[member] * grad_mag)
        relaxed = flow_pops[member] - omega * (flow_pops[member] - balance) + perturb
        results.append(jnp.where(fluid, relaxed, flow_pops[member]))
    sharpen_coef = 0.7 * (1.0 - phase * phase) / grad_mag
    for member in range(7):
        offset = VEL_F[member]
        along = offset[0] * flow[0] + offset[1] * flow[1] + offset[2] * flow[2]
        cross = offset[0] * grads[0] + offset[1] * grads[1] + offset[2] * grads[2]
        balance = WT_G[member] * (phase * (1.0 + 4.0 * along) + sharpen_coef * cross)
        relaxed = phase_pops[member] - 1.25 * (phase_pops[member] - balance)
        results.append(jnp.where(fluid, relaxed, phase_pops[member]))
    return jnp.stack(results)

def window(field, flags, offset, sizes):
    starts = [1 - offset[dim] if flags[dim] else 0 for dim in range(3)]
    return field[starts[0]:starts[0] + sizes[0], starts[1]:starts[1] + sizes[1], starts[2]:starts[2] + sizes[2]]

def propagate(post, source, fluid_pad, fluid):
    sizes = post.shape[1:]
    results = []
    for member in range(26):
        offset = VEL_ALL[member]
        field, flags = source(member)
        source_vals = window(field, flags, offset, sizes)
        source_fluid = window(fluid_pad, (1, 1, 1), offset, sizes) == 1
        moved = jnp.where(source_fluid, source_vals, post[OPP_ALL[member]])
        results.append(jnp.where(fluid, moved, post[member]))
    return jnp.stack(results)

def gradient(padded):
    grad_x = 0.5 * (padded[2:, 1:-1, 1:-1] - padded[:-2, 1:-1, 1:-1])
    grad_y = 0.5 * (padded[1:-1, 2:, 1:-1] - padded[1:-1, :-2, 1:-1])
    grad_z = 0.5 * (padded[1:-1, 1:-1, 2:] - padded[1:-1, 1:-1, :-2])
    return (grad_x, grad_y, grad_z)

def reference(flow_pops, phase_pops, pore_mask):
    fluid_pad = jnp.pad(pore_mask, 1)
    fluid = pore_mask == 1
    for step in range(STEPS):
        phase = lax.optimization_barrier(jnp.sum(phase_pops, axis=0))
        padded = jnp.pad(jnp.where(fluid, phase, jnp.float32(0.0)), 1)
        post = relax(flow_pops, phase_pops, phase, gradient(padded), fluid)
        full = jnp.pad(post, ((0, 0), (1, 1), (1, 1), (1, 1)))

        def source(member):
            return (full[member], (1, 1, 1))
        moved = propagate(post, source, fluid_pad, fluid)
        flow_pops = moved[:19]
        phase_pops = moved[19:]
    return (flow_pops, phase_pops)
```

```python
import itertools

import jax
import jax.numpy as jnp
from jax import lax
from jax.experimental import pallas as pl
from jax.experimental.pallas import tpu as pltpu
from jax.sharding import PartitionSpec as P

STEPS = 2
MESH = pl.DeviceIdType.MESH
AXES = ("gx", "gy", "gz")
VEL = [
    (0, 0, 0),
    (1, 0, 0),
    (-1, 0, 0),
    (0, 1, 0),
    (0, -1, 0),
    (0, 0, 1),
    (0, 0, -1),
    (1, 1, 0),
    (-1, -1, 0),
    (1, -1, 0),
    (-1, 1, 0),
    (1, 0, 1),
    (-1, 0, -1),
    (1, 0, -1),
    (-1, 0, 1),
    (0, 1, 1),
    (0, -1, -1),
    (0, 1, -1),
    (0, -1, 1),
]
INDEX = {c: i for i, c in enumerate(VEL)}
OPP = [0, 2, 1, 4, 3, 6, 5, 8, 7, 10, 9, 12, 11, 14, 13, 16, 15, 18, 17]
VEL_ALL = VEL + VEL[:7]
OPP_ALL = OPP + [19 + j for j in OPP[:7]]
WT = [1.0 / 3.0] + [1.0 / 18.0] * 6 + [1.0 / 36.0] * 12
BT = [-2.0 / 9.0] + [1.0 / 54.0] * 6 + [1.0 / 27.0] * 12
OFFS = sorted(
    (o for o in itertools.product((-1, 0, 1), repeat=3) if any(o)),
    key=lambda o: -sum(map(abs, o)),
)
SLOT = {o: n for n, o in enumerate(OFFS)}


def neg(o):
    return tuple(-d for d in o)


def crossing(dim, sign):
    flow = [i for i in range(19) if VEL[i][dim] == sign]
    return flow + [19 + INDEX[tuple(sign if d == dim else 0 for d in range(3))]]


def iota(dim):
    return lax.broadcasted_iota(jnp.int32, (1, 8, 128), dim)


def roll(v, shift, axis):
    size = v.shape[axis]
    shift %= size
    return pltpu.roll(v, shift, axis) if shift else v


def rows(v, frm, to):
    return roll(v, to - frm, 1)


def lanes(v, frm, to):
    return roll(v, to - frm, 2)


def sel(mask, a, b):
    return jnp.where(jnp.broadcast_to(mask, a.shape), a, b)


def local_part(pops, fluid):
    f, g = pops[:19], pops[19:]
    phase = ((g[0] + g[1]) + (g[2] + g[3])) + ((g[4] + g[5]) + g[6])
    masked = jnp.where(fluid, phase, 0.0)
    sums = {i: f[i] + f[OPP[i]] for i in range(1, 19, 2)}
    diff = {i: f[i] - f[OPP[i]] for i in range(1, 19, 2)}
    density = f[0]
    for i in range(1, 19, 2):
        density = density + sums[i]
    inv = 1.0 / density
    mom = []
    for dim in range(3):
        total = None
        for i in range(1, 19, 2):
            s = VEL[i][dim]
            if s:
                term = diff[i]
                total = term if total is None else (total + term if s > 0 else total - term)
        mom.append(total)
    flow = [m * inv for m in mom]
    speed_sq = flow[0] * flow[0] + flow[1] * flow[1] + flow[2] * flow[2]
    omega = 1.0 / (0.8 + 0.2 * phase)
    keep = 1.0 - omega
    base = omega * density
    even0 = base * (1.0 - 1.5 * speed_sq)
    out = [None] * 26
    out[0] = keep * f[0] + WT[0] * even0
    for i in range(1, 19, 2):
        c = VEL[i]
        along = None
        for dim in range(3):
            if c[dim]:
                term = flow[dim]
                along = term if along is None else (along + term if c[dim] > 0 else along - term)
        even = WT[i] * even0 + (4.5 * WT[i]) * base * (along * along)
        odd = (3.0 * WT[i]) * base * along
        out[i] = keep * f[i] + (even + odd)
        out[i + 1] = keep * f[i + 1] + (even - odd)
    out[19] = (1.25 * 0.25) * phase - 0.25 * g[0]
    eighth = (1.25 * 0.125) * phase
    for dim in range(3):
        odd = 4.0 * eighth * flow[dim]
        out[20 + 2 * dim] = (eighth + odd) - 0.25 * g[1 + 2 * dim]
        out[21 + 2 * dim] = (eighth - odd) - 0.25 * g[2 + 2 * dim]
    return out, phase, masked


def fill_messages(stage, local, masked, solid):
    row, lane = iota(1), iota(2)
    for side, sign in ((0, -1), (1, 1)):
        near, far = (3, 2) if side else (0, 1)
        out = stage["x"]
        for k, i in enumerate(crossing(0, sign)):
            out[side, k] = local[i][near]
        out[side, 6] = masked[near]
        out[side, 7] = masked[far]
        if solid is not None:
            out[side, 8] = solid[near]
        acc = masked
        edge, first = (7, 0) if side else (0, 2)
        for k, i in enumerate(crossing(1, sign)):
            acc = sel(row == first + k, rows(local[i], edge, first + k), acc)
        stage["y"][side, 0] = acc
        if solid is not None:
            stage["y"][side, 1] = solid
        acc = masked
        edge = 127 if side else 0
        for k, i in enumerate(crossing(2, sign)):
            acc = sel(lane == first + k, lanes(local[i], edge, first + k), acc)
        if solid is not None:
            acc = sel(lane == first + 6, lanes(solid, edge, first + 6), acc)
        stage["z"][side] = acc
    for sa, sb in itertools.product((0, 1), repeat=2):
        near, far = (3, 2) if sa else (0, 1)
        xs, fs = slice(near, near + 1), slice(far, far + 1)
        ga, gb = 2 * sa - 1, 2 * sb - 1
        acc = masked[xs]
        edge, pop, flag, deep = (7, 3, 2, 4) if sb else (0, 4, 5, 3)
        acc = sel(row == pop, rows(local[INDEX[(ga, gb, 0)]][xs], edge, pop), acc)
        acc = sel(row == deep, rows(masked[fs], edge, deep), acc)
        if solid is not None:
            acc = sel(row == flag, rows(solid[xs], edge, flag), acc)
        stage["xy"][sa, sb] = acc
        acc = masked[xs]
        edge, pop, flag, deep = (127, 63, 62, 61) if sb else (0, 64, 65, 66)
        acc = sel(lane == pop, lanes(local[INDEX[(ga, 0, gb)]][xs], edge, pop), acc)
        acc = sel(lane == deep, lanes(masked[fs], edge, deep), acc)
        if solid is not None:
            acc = sel(lane == flag, lanes(solid[xs], edge, flag), acc)
        stage["xz"][sa, sb] = acc
        acc = masked
        edge, pop, flag = (7, 3, 2) if sa else (0, 4, 5)
        acc = sel(row == pop, rows(local[INDEX[(0, ga, gb)]], edge, pop), acc)
        if solid is not None:
            acc = sel(row == flag, rows(solid, edge, flag), acc)
        stage["yz"][sa, sb] = acc
    stage["c"][0] = masked[0:1]
    stage["c"][1] = masked[3:4]


def part(bufs, o, first):
    a, b, c = ((d + 1) // 2 for d in o)
    kind = tuple(d != 0 for d in o)
    if kind == (True, False, False):
        return bufs["x"].at[a, pl.ds(0, 9 if first else 8)]
    if kind == (False, True, False):
        return bufs["y"].at[b, pl.ds(0, 2 if first else 1)]
    if kind == (False, False, True):
        return bufs["z"].at[c]
    if kind == (True, True, False):
        return bufs["xy"].at[a, b]
    if kind == (True, False, True):
        return bufs["xz"].at[a, c]
    if kind == (False, True, True):
        return bufs["yz"].at[b, c]
    return bufs["c"].at[a, b, c]


def pair_shift(own, halo, sign, axis):
    size = own.shape[axis]
    at = iota(axis)
    if sign > 0:
        return sel(at == 0, roll(halo, 1, axis), roll(own, 1, axis))
    return sel(at == size - 1, roll(halo, -1, axis), roll(own, -1, axis))


def shift(c, t00, t10, t01, t11):
    if c[1]:
        t00 = pair_shift(t00(), t10(), c[1], 1)
        halo = (lambda: pair_shift(t01(), t11(), c[1], 1)) if c[2] else None
    else:
        t00, halo = t00(), t01
    return pair_shift(t00, halo(), c[2], 2) if c[2] else t00


def join(*parts):
    return jnp.concatenate(parts, axis=0)


def minus_plus(minus, plus, axis):
    at = iota(axis)
    half = 4 if axis == 1 else 64
    return sel(at < half, plus, minus)


def along_x(c, own, low, high):
    if c[0] > 0:
        return join(low(), own[0:3])
    if c[0] < 0:
        return join(own[1:4], high())
    return own


def source_flags(recv, solid):
    y = minus_plus(recv["y"][0, 1], recv["y"][1, 1], 1)
    z = minus_plus(lanes(recv["z"][0], 6, 127), lanes(recv["z"][1], 8, 0), 2)
    x = [recv["x"][s, 8:9] for s in (0, 1)]
    xy = [
        minus_plus(rows(recv["xy"][s, 0], 2, 7), rows(recv["xy"][s, 1], 5, 0), 1) for s in (0, 1)
    ]
    xz = [
        minus_plus(lanes(recv["xz"][s, 0], 62, 127), lanes(recv["xz"][s, 1], 65, 0), 2)
        for s in (0, 1)
    ]
    yz = [
        minus_plus(rows(recv["yz"][0, s], 2, 7), rows(recv["yz"][1, s], 5, 0), 1) for s in (0, 1)
    ]
    yz = minus_plus(yz[0], yz[1], 2)
    flags = []
    for i in range(1, 19):
        c = VEL[i]
        flags.append(
            shift(
                c,
                lambda: along_x(c, solid, lambda: x[0], lambda: x[1]),
                lambda: along_x(c, y, lambda: xy[0], lambda: xy[1]),
                lambda: along_x(c, z, lambda: xz[0], lambda: xz[1]),
                lambda: yz,
            )
        )
    return flags


def finish_step(recv, pops, local, masked, fluid, flag):
    rx, ry, rz = recv["x"], recv["y"], recv["z"]
    rxy, rxz, ryz, rc = recv["xy"], recv["xz"], recv["yz"], recv["c"]

    def deep_xy(s):
        return minus_plus(rows(rxy[s, 0], 4, 7), rows(rxy[s, 1], 3, 0), 1)

    def deep_xz(s):
        return minus_plus(lanes(rxz[s, 0], 61, 127), lanes(rxz[s, 1], 66, 0), 2)

    def near_xy(s):
        return minus_plus(rxy[s, 0], rxy[s, 1], 1)

    def near_xz(s):
        return minus_plus(rxz[s, 0], rxz[s, 1], 2)

    def corner(s):
        return minus_plus(
            minus_plus(rc[s, 0, 0], rc[s, 0, 1], 2), minus_plus(rc[s, 1, 0], rc[s, 1, 1], 2), 1
        )

    m00 = join(rx[0, 7:8], rx[0, 6:7], masked, rx[1, 6:7], rx[1, 7:8])
    m10 = join(
        deep_xy(0), near_xy(0), minus_plus(ry[0, 0], ry[1, 0], 1), near_xy(1), deep_xy(1)
    )
    m01 = join(deep_xz(0), near_xz(0), minus_plus(rz[0], rz[1], 2), near_xz(1), deep_xz(1))
    m11 = join(
        corner(0),
        minus_plus(
            minus_plus(ryz[0, 0], ryz[0, 1], 2), minus_plus(ryz[1, 0], ryz[1, 1], 2), 1
        ),
        corner(1),
    )

    def grads(own, in_y, in_z):
        mid = own[1:-1]
        gx = 0.5 * (own[2:] - own[:-2])
        gy = 0.5 * (pair_shift(mid, in_y, -1, 1) - pair_shift(mid, in_y, 1, 1))
        gz = 0.5 * (pair_shift(mid, in_z, -1, 2) - pair_shift(mid, in_z, 1, 2))
        square = gx * gx + gy * gy + gz * gz + 0.01
        inv = lax.rsqrt(square)
        return ((gx, gy, gz), inv, square * inv, mid)

    tiles = {
        "00": grads(m00, m10[1:-1], m01[1:-1]),
        "10": grads(m10, m00[1:-1], m11),
        "01": grads(m01, m11, m00[1:-1]),
        "11": grads(m11, m01[2:-2], m10[2:-2]),
    }
    known = {}

    def cut(v, name, lo, hi):
        base = 0 if name == "11" else -1
        return v[lo - base : hi - base + 1]

    def term(i, name, lo, hi):
        grad, inv, mag, phase = tiles[name]
        if i >= 19:
            dim, sign = (i - 20) // 2, 1 - 2 * ((i - 20) % 2)
            key = ("g", dim, name, lo, hi)
            if key not in known:
                p, d, r = (cut(v, name, lo, hi) for v in (phase, grad[dim], inv))
                known[key] = (0.875 * 0.125) * ((1.0 - p * p) * (d * r))
            return known[key] if sign > 0 else -known[key]
        pair = i if i % 2 else i - 1
        key = (pair, name, lo, hi)
        if key not in known:
            cross = None
            for dim in range(3):
                if VEL[pair][dim]:
                    d = cut(grad[dim], name, lo, hi)
                    cross = (
                        d if cross is None else (cross + d if VEL[pair][dim] > 0 else cross - d)
                    )
            r, m = cut(inv, name, lo, hi), cut(mag, name, lo, hi)
            known[key] = (0.5 * WT[pair]) * (cross * cross * r) - (0.5 * BT[pair]) * m
        return known[key]

    post = [None] * 26
    post[0] = local[0] - (0.5 * BT[0]) * cut(tiles["00"][2], "00", 0, 3)
    post[19] = local[19]
    for i in itertools.chain(range(1, 19), range(20, 26)):
        post[i] = local[i] + term(i, "00", 0, 3)

    results = []
    for i in range(26):
        if i in (0, 19):
            results.append(jnp.where(fluid, post[i], pops[i]))
            continue
        c = VEL_ALL[i]
        lo, hi = -c[0], 3 - c[0]
        sx, sy, sz = ((1 - d) // 2 for d in c)

        def from_x():
            k = crossing(0, c[0]).index(i)
            return rx[sx, k : k + 1] + term(i, "00", 4 * sx + sx - 1, 4 * sx + sx - 1)

        def t00():
            return along_x(c, post[i], from_x, from_x)

        def t10():
            k = crossing(1, c[1]).index(i)
            packed = rows(ry[sy, 0], k, 7) if sy == 0 else rows(ry[sy, 0], k + 2, 0)

            def edge():
                return rows(rxy[sx, sy], 3, 7) if sy == 0 else rows(rxy[sx, sy], 4, 0)

            return along_x(c, packed, edge, edge) + term(i, "10", lo, hi)

        def t01():
            k = crossing(2, c[2]).index(i)
            packed = lanes(rz[sz], k, 127) if sz == 0 else lanes(rz[sz], k + 2, 0)

            def edge():
                return lanes(rxz[sx, sz], 63, 127) if sz == 0 else lanes(rxz[sx, sz], 64, 0)

            return along_x(c, packed, edge, edge) + term(i, "01", lo, hi)

        def t11():
            packed = rows(ryz[sy, sz], 3, 7) if sy == 0 else rows(ryz[sy, sz], 4, 0)
            return packed + term(i, "11", lo, hi)

        came = shift(c, t00, t10, t01, t11)
        back = jnp.where(fluid, post[OPP_ALL[i]], pops[i])
        results.append(jnp.where(flag(i if i < 19 else i - 19), came, back))
    return results


KINDS = {
    "x": (2, 9, 8, 128),
    "y": (2, 2, 4, 8, 128),
    "z": (2, 4, 8, 128),
    "xy": (2, 2, 1, 8, 128),
    "xz": (2, 2, 1, 8, 128),
    "yz": (2, 2, 4, 8, 128),
    "c": (2, 2, 2, 1, 8, 128),
}


def kernel(counts, flow_hbm, phase_hbm, mask_hbm, flow_out, phase_out, *scratch):
    flow_in, phase_in, mask_in, flags, load_sem, send_sem, recv_sem = scratch[:7]
    names = list(KINDS)
    stage_refs = dict(zip(names, scratch[7:14]))
    recv_refs = dict(zip(names, scratch[14:21]))
    loads = [
        pltpu.make_async_copy(src, dst, load_sem.at[n])
        for n, (src, dst) in enumerate(
            ((phase_hbm, phase_in), (mask_hbm, mask_in), (flow_hbm, flow_in))
        )
    ]
    for load in loads:
        load.start()
    at = [lax.axis_index(a) for a in AXES]

    def exists(o):
        ok = None
        for dim, d in enumerate(o):
            if d:
                here = at[dim] > 0 if d < 0 else at[dim] < counts[dim] - 1
                ok = here if ok is None else jnp.logical_and(ok, here)
        return ok

    def peer(o):
        return tuple(at[dim] + d for dim, d in enumerate(o))

    for o in OFFS:

        @pl.when(jnp.logical_not(exists(o)))
        def _(o=o):
            for step in range(STEPS):
                ref = part({k: r.at[step] for k, r in recv_refs.items()}, o, True)
                ref[...] = jnp.zeros(ref.shape, jnp.float32)

    barrier = pltpu.get_barrier_semaphore()
    for o in OFFS:

        @pl.when(exists(o))
        def _(o=o):
            pl.semaphore_signal(barrier, inc=1, device_id=peer(o), device_id_type=MESH)

    near = 1
    for dim in range(3):
        near = near * (
            1
            + (at[dim] > 0).astype(jnp.int32)
            + (at[dim] < counts[dim] - 1).astype(jnp.int32)
        )

    def copy(step, o):
        stage = {k: r.at[step] for k, r in stage_refs.items() if k != "c"}
        recv = {k: r.at[step] for k, r in recv_refs.items()}
        first = step == 0
        if all(o):
            src = stage_refs["c"].at[step, (o[0] + 1) // 2]
        else:
            src = part(stage, o, first)
        return pltpu.make_async_remote_copy(
            src_ref=src,
            dst_ref=part(recv, neg(o), first),
            send_sem=send_sem.at[step, SLOT[o]],
            recv_sem=recv_sem.at[step, SLOT[neg(o)]],
            device_id=peer(o),
            device_id_type=MESH,
        )

    for load in loads:
        load.wait()
    fluid = mask_in[...] == 1
    solid = jnp.where(fluid, 1.0, 0.0)
    pops = [flow_in[i] for i in range(19)] + [phase_in[j] for j in range(7)]
    for step in range(STEPS):
        stage = {k: r.at[step] for k, r in stage_refs.items()}
        recv = {k: r.at[step] for k, r in recv_refs.items()}
        local, _, masked = local_part(pops, fluid)
        fill_messages(stage, local, masked, solid if step == 0 else None)
        if step == 0:
            pl.semaphore_wait(barrier, near - 1)
        for o in OFFS:

            @pl.when(exists(o))
            def _(o=o, step=step):
                copy(step, o).start()

        for o in OFFS:

            @pl.when(exists(o))
            def _(o=o, step=step):
                here = part(recv, o, step == 0)
                pltpu.make_async_remote_copy(
                    src_ref=here,
                    dst_ref=here,
                    send_sem=send_sem.at[step, SLOT[o]],
                    recv_sem=recv_sem.at[step, SLOT[o]],
                    device_id=peer(o),
                    device_id_type=MESH,
                ).wait_recv()

        if step == 0:
            for n, value in enumerate(source_flags(recv, solid)):
                flags[n] = jnp.where(fluid, value, 0.0)
        pops = finish_step(recv, pops, local, masked, fluid, lambda i: flags[i - 1] > 0.5)
    for i in range(19):
        flow_out[i] = pops[i]
    for j in range(7):
        phase_out[j] = pops[19 + j]
    for step in range(STEPS):
        for o in OFFS:

            @pl.when(exists(o))
            def _(o=o, step=step):
                copy(step, o).wait_send()


def solution(mesh):
    counts = [mesh.shape[a] for a in AXES]

    def shards(flow_pops, phase_pops, pore_mask):
        f32 = jnp.float32
        stage_kinds = dict(KINDS, c=(2, 1, 8, 128))
        return pl.pallas_call(
            lambda *refs: kernel(counts, *refs),
            out_shape=(
                jax.ShapeDtypeStruct(flow_pops.shape, f32),
                jax.ShapeDtypeStruct(phase_pops.shape, f32),
            ),
            in_specs=[pl.BlockSpec(memory_space=pl.ANY)] * 3,
            out_specs=(pl.BlockSpec(memory_space=pltpu.VMEM),) * 2,
            scratch_shapes=[
                pltpu.VMEM((19, 4, 8, 128), f32),
                pltpu.VMEM((7, 4, 8, 128), f32),
                pltpu.VMEM((4, 8, 128), jnp.int32),
                pltpu.VMEM((18, 4, 8, 128), f32),
                pltpu.SemaphoreType.DMA((3,)),
                pltpu.SemaphoreType.DMA((STEPS, 26)),
                pltpu.SemaphoreType.DMA((STEPS, 26)),
            ]
            + [pltpu.VMEM((STEPS, *shape), f32) for shape in stage_kinds.values()]
            + [pltpu.VMEM((STEPS, *shape), f32) for shape in KINDS.values()],
            compiler_params=pltpu.CompilerParams(
                collective_id=0, has_side_effects=True, vmem_limit_bytes=32 << 20
            ),
            name="lattice_steps",
        )(flow_pops, phase_pops, pore_mask)

    return jax.shard_map(
        shards,
        mesh=mesh,
        in_specs=(P(None, *AXES), P(None, *AXES), P(*AXES)),
        out_specs=(P(None, *AXES), P(None, *AXES)),
        check_vma=False,
    )
```

```python
import itertools

import jax
import jax.numpy as jnp
from jax import lax
from jax.experimental import pallas as pl
from jax.experimental.pallas import tpu as pltpu
from jax.sharding import PartitionSpec as P

STEPS = 2
MESH = pl.DeviceIdType.MESH
AXES = ("gx", "gy", "gz")
VEL = [
    (0, 0, 0),
    (1, 0, 0),
    (-1, 0, 0),
    (0, 1, 0),
    (0, -1, 0),
    (0, 0, 1),
    (0, 0, -1),
    (1, 1, 0),
    (-1, -1, 0),
    (1, -1, 0),
    (-1, 1, 0),
    (1, 0, 1),
    (-1, 0, -1),
    (1, 0, -1),
    (-1, 0, 1),
    (0, 1, 1),
    (0, -1, -1),
    (0, 1, -1),
    (0, -1, 1),
]
INDEX = {c: i for i, c in enumerate(VEL)}
OPP = [0, 2, 1, 4, 3, 6, 5, 8, 7, 10, 9, 12, 11, 14, 13, 16, 15, 18, 17]
VEL_ALL = VEL + VEL[:7]
OPP_ALL = OPP + [19 + j for j in OPP[:7]]
WT = [1.0 / 3.0] + [1.0 / 18.0] * 6 + [1.0 / 36.0] * 12
BT = [-2.0 / 9.0] + [1.0 / 54.0] * 6 + [1.0 / 27.0] * 12
OFFS = sorted(
    (o for o in itertools.product((-1, 0, 1), repeat=3) if any(o)),
    key=lambda o: -sum(map(abs, o)),
)
SLOT = {o: n for n, o in enumerate(OFFS)}


def neg(o):
    return tuple(-d for d in o)


def crossing(dim, sign):
    flow = [i for i in range(19) if VEL[i][dim] == sign]
    return flow + [19 + INDEX[tuple(sign if d == dim else 0 for d in range(3))]]


def iota(dim):
    return lax.broadcasted_iota(jnp.int32, (1, 8, 128), dim)


def roll(v, shift, axis):
    size = v.shape[axis]
    shift %= size
    return pltpu.roll(v, shift, axis) if shift else v


def rows(v, frm, to):
    return roll(v, to - frm, 1)


def lanes(v, frm, to):
    return roll(v, to - frm, 2)


def sel(mask, a, b):
    return jnp.where(jnp.broadcast_to(mask, a.shape), a, b)


def local_part(pops, fluid):
    f, g = pops[:19], pops[19:]
    phase = ((g[0] + g[1]) + (g[2] + g[3])) + ((g[4] + g[5]) + g[6])
    masked = jnp.where(fluid, phase, 0.0)
    sums = {i: f[i] + f[OPP[i]] for i in range(1, 19, 2)}
    diff = {i: f[i] - f[OPP[i]] for i in range(1, 19, 2)}
    density = f[0]
    for i in range(1, 19, 2):
        density = density + sums[i]
    inv = 1.0 / density
    mom = []
    for dim in range(3):
        total = None
        for i in range(1, 19, 2):
            s = VEL[i][dim]
            if s:
                term = diff[i]
                total = term if total is None else (total + term if s > 0 else total - term)
        mom.append(total)
    flow = [m * inv for m in mom]
    speed_sq = flow[0] * flow[0] + flow[1] * flow[1] + flow[2] * flow[2]
    omega = 1.0 / (0.8 + 0.2 * phase)
    keep = 1.0 - omega
    base = omega * density
    even0 = base * (1.0 - 1.5 * speed_sq)
    out = [None] * 26
    out[0] = keep * f[0] + WT[0] * even0
    for i in range(1, 19, 2):
        c = VEL[i]
        along = None
        for dim in range(3):
            if c[dim]:
                term = flow[dim]
                along = term if along is None else (along + term if c[dim] > 0 else along - term)
        even = WT[i] * even0 + (4.5 * WT[i]) * base * (along * along)
        odd = (3.0 * WT[i]) * base * along
        out[i] = keep * f[i] + (even + odd)
        out[i + 1] = keep * f[i + 1] + (even - odd)
    out[19] = (1.25 * 0.25) * phase - 0.25 * g[0]
    eighth = (1.25 * 0.125) * phase
    for dim in range(3):
        odd = 4.0 * eighth * flow[dim]
        out[20 + 2 * dim] = (eighth + odd) - 0.25 * g[1 + 2 * dim]
        out[21 + 2 * dim] = (eighth - odd) - 0.25 * g[2 + 2 * dim]
    return out, phase, masked


def merge_planes(v, block, offset):
    lane = iota(2)
    acc = roll(v[0:1], offset, 2)
    for x in range(1, 4):
        acc = sel(lane >= block * x, roll(v[x : x + 1], block * x + offset, 2), acc)
    return acc


def split_planes(v, block, offset):
    return join(*(roll(v, -(block * x + offset), 2) for x in range(4)))


def fill_corners_and_edges(stage, local, masked, solid):
    row, lane = iota(1), iota(2)
    for sa, sb in itertools.product((0, 1), repeat=2):
        near, far = (3, 2) if sa else (0, 1)
        xs, fs = slice(near, near + 1), slice(far, far + 1)
        ga, gb = 2 * sa - 1, 2 * sb - 1
        edge = 7 if sb else 0
        stage["c"][sa, sb] = masked[near][edge : edge + 1]
        acc = masked
        edge, pop, flag = (7, 3, 2) if sa else (0, 4, 5)
        acc = sel(row == pop, rows(local[INDEX[(0, ga, gb)]], edge, pop), acc)
        if solid is not None:
            acc = sel(row == flag, rows(solid, edge, flag), acc)
        stage["yz"][sa, sb] = merge_planes(acc, 2, 2 * sb)
        acc = masked[xs]
        edge, pop, flag, deep = (127, 63, 62, 61) if sb else (0, 64, 65, 66)
        acc = sel(lane == pop, lanes(local[INDEX[(ga, 0, gb)]][xs], edge, pop), acc)
        acc = sel(lane == deep, lanes(masked[fs], edge, deep), acc)
        if solid is not None:
            acc = sel(lane == flag, lanes(solid[xs], edge, flag), acc)
        stage["xz"][sa, sb] = acc
        acc = masked[xs]
        edge, pop, flag, deep = (7, 3, 2, 4) if sb else (0, 4, 5, 3)
        acc = sel(row == pop, rows(local[INDEX[(ga, gb, 0)]][xs], edge, pop), acc)
        acc = sel(row == deep, rows(masked[fs], edge, deep), acc)
        if solid is not None:
            acc = sel(row == flag, rows(solid[xs], edge, flag), acc)
        stage["xy"][sa, sb] = acc


def fill_faces(stage, local, masked, solid):
    row, lane = iota(1), iota(2)
    for side, sign in ((0, -1), (1, 1)):
        near, far = (3, 2) if side else (0, 1)
        acc = masked
        edge, first = (127, 0) if side else (0, 2)
        for k, i in enumerate(crossing(2, sign)):
            acc = sel(lane == first + k, lanes(local[i], edge, first + k), acc)
        if solid is not None:
            acc = sel(lane == first + 6, lanes(solid, edge, first + 6), acc)
        stage["z"][side] = merge_planes(acc, 16, 2 * side)
        acc = masked
        edge, first = (7, 0) if side else (0, 2)
        for k, i in enumerate(crossing(1, sign)):
            acc = sel(row == first + k, rows(local[i], edge, first + k), acc)
        stage["y"][side, 0:4] = acc
        if solid is not None:
            acc = rows(solid[0:1], edge, 0)
            for x in range(1, 4):
                acc = sel(row == x, rows(solid[x : x + 1], edge, x), acc)
            stage["y"][side, 4:5] = acc
        out = stage["x"]
        for k, i in enumerate(crossing(0, sign)):
            out[side, k] = local[i][near]
        out[side, 6] = masked[near]
        out[side, 7] = masked[far]
        if solid is not None:
            out[side, 8] = solid[near]


def part(bufs, o, first):
    a, b, c = ((d + 1) // 2 for d in o)
    kind = tuple(d != 0 for d in o)
    if kind == (True, False, False):
        return bufs["x"].at[a, pl.ds(0, 9 if first else 8)]
    if kind == (False, True, False):
        return bufs["y"].at[b, pl.ds(0, 5 if first else 4)]
    if kind == (False, False, True):
        return bufs["z"].at[c]
    if kind == (True, True, False):
        return bufs["xy"].at[a, b]
    if kind == (True, False, True):
        return bufs["xz"].at[a, c]
    if kind == (False, True, True):
        return bufs["yz"].at[b, c]
    return bufs["c"].at[a, b, c]


def pair_shift(own, halo, sign, axis):
    size = own.shape[axis]
    at = iota(axis)
    if sign > 0:
        return sel(at == 0, roll(halo, 1, axis), roll(own, 1, axis))
    return sel(at == size - 1, roll(halo, -1, axis), roll(own, -1, axis))


def shift(c, t00, t10, t01, t11):
    if c[1]:
        t00 = pair_shift(t00(), t10(), c[1], 1)
        halo = (lambda: pair_shift(t01(), t11(), c[1], 1)) if c[2] else None
    else:
        t00, halo = t00(), t01
    return pair_shift(t00, halo(), c[2], 2) if c[2] else t00


def join(*parts):
    return jnp.concatenate(parts, axis=0)


def minus_plus(minus, plus, axis):
    at = iota(axis)
    half = 4 if axis == 1 else 64
    return sel(at < half, plus, minus)


def along_x(c, own, low, high):
    if c[0] > 0:
        return join(low(), own[0:3])
    if c[0] < 0:
        return join(own[1:4], high())
    return own


def source_flags(recv, solid):
    y = [recv["y"][s, 4:5] for s in (0, 1)]
    y = join(*(minus_plus(rows(y[0], x, 7), rows(y[1], x, 0), 1) for x in range(4)))
    z = [split_planes(recv["z"][s], 16, 2 * (1 - s)) for s in (0, 1)]
    z = minus_plus(lanes(z[0], 6, 127), lanes(z[1], 8, 0), 2)
    x = [recv["x"][s, 8:9] for s in (0, 1)]
    xy = [
        minus_plus(rows(recv["xy"][s, 0], 2, 7), rows(recv["xy"][s, 1], 5, 0), 1) for s in (0, 1)
    ]
    xz = [
        minus_plus(lanes(recv["xz"][s, 0], 62, 127), lanes(recv["xz"][s, 1], 65, 0), 2)
        for s in (0, 1)
    ]
    yz = [
        minus_plus(rows(recv["yz"][0, s], 2, 7), rows(recv["yz"][1, s], 5, 0), 1) for s in (0, 1)
    ]
    yz = [split_planes(yz[s], 2, 2 * (1 - s)) for s in (0, 1)]
    yz = minus_plus(yz[0], yz[1], 2)
    flags = []
    for i in range(1, 19):
        c = VEL[i]
        flags.append(
            shift(
                c,
                lambda: along_x(c, solid, lambda: x[0], lambda: x[1]),
                lambda: along_x(c, y, lambda: xy[0], lambda: xy[1]),
                lambda: along_x(c, z, lambda: xz[0], lambda: xz[1]),
                lambda: yz,
            )
        )
    return flags


def finish_step(recv, pops, local, masked, fluid, wait_faces, wait_rest):
    def grads(own, in_y, in_z):
        mid = own[1:-1]
        gx = 0.5 * (own[2:] - own[:-2])
        gy = 0.5 * (pair_shift(mid, in_y, -1, 1) - pair_shift(mid, in_y, 1, 1))
        gz = 0.5 * (pair_shift(mid, in_z, -1, 2) - pair_shift(mid, in_z, 1, 2))
        square = gx * gx + gy * gy + gz * gz + 0.01
        inv = lax.rsqrt(square)
        return ((gx, gy, gz), inv, square * inv, mid)

    tiles, known = {}, {}
    first_plane = {"00": 0, "low": -1, "high": 4, "10": -1, "01": -1, "11": 0}

    def cut(v, name, lo, hi):
        base = first_plane[name]
        return v[lo - base : hi - base + 1]

    def term(i, name, lo, hi):
        grad, inv, mag, phase = tiles[name]
        if i >= 19:
            dim, sign = (i - 20) // 2, 1 - 2 * ((i - 20) % 2)
            key = ("g", dim, name, lo, hi)
            if key not in known:
                p, d, r = (cut(v, name, lo, hi) for v in (phase, grad[dim], inv))
                known[key] = (0.875 * 0.125) * ((1.0 - p * p) * (d * r))
            return known[key] if sign > 0 else -known[key]
        pair = i if i % 2 else i - 1
        key = (pair, name, lo, hi)
        if key not in known:
            cross = None
            for dim in range(3):
                if VEL[pair][dim]:
                    d = cut(grad[dim], name, lo, hi)
                    cross = (
                        d if cross is None else (cross + d if VEL[pair][dim] > 0 else cross - d)
                    )
            r, m = cut(inv, name, lo, hi), cut(mag, name, lo, hi)
            known[key] = (0.5 * WT[pair]) * (cross * cross * r) - (0.5 * BT[pair]) * m
        return known[key]

    wait_faces()
    rx, ry = recv["x"], recv["y"]
    rz = [split_planes(recv["z"][s], 16, 2 * (1 - s)) for s in (0, 1)]
    y_faces = [ry[s, 0:4] for s in (0, 1)]
    m00 = join(rx[0, 7:8], rx[0, 6:7], masked, rx[1, 6:7], rx[1, 7:8])
    m10 = minus_plus(y_faces[0], y_faces[1], 1)
    m01 = minus_plus(rz[0], rz[1], 2)
    tiles["00"] = grads(m00[1:-1], m10, m01)
    post = [None] * 26
    post[0] = local[0] - (0.5 * BT[0]) * tiles["00"][2]
    post[19] = local[19]
    for i in itertools.chain(range(1, 19), range(20, 26)):
        post[i] = local[i] + term(i, "00", 0, 3)

    flag = wait_rest()
    rxy, rxz, rc = recv["xy"], recv["xz"], recv["c"]
    ryz = [[split_planes(recv["yz"][b, c], 2, 2 * (1 - c)) for c in (0, 1)] for b in (0, 1)]

    def deep_xy(s):
        return minus_plus(rows(rxy[s, 0], 4, 7), rows(rxy[s, 1], 3, 0), 1)

    def deep_xz(s):
        return minus_plus(lanes(rxz[s, 0], 61, 127), lanes(rxz[s, 1], 66, 0), 2)

    def near_xy(s):
        return minus_plus(rxy[s, 0], rxy[s, 1], 1)

    def near_xz(s):
        return minus_plus(rxz[s, 0], rxz[s, 1], 2)

    def corner(s):
        line = [[jnp.broadcast_to(rc[s, b, c][None], (1, 8, 128)) for c in (0, 1)] for b in (0, 1)]
        return minus_plus(minus_plus(*line[0], 2), minus_plus(*line[1], 2), 1)

    m10 = join(deep_xy(0), near_xy(0), m10, near_xy(1), deep_xy(1))
    m01 = join(deep_xz(0), near_xz(0), m01, near_xz(1), deep_xz(1))
    m11 = join(
        corner(0), minus_plus(minus_plus(*ryz[0], 2), minus_plus(*ryz[1], 2), 1), corner(1)
    )
    tiles["low"] = grads(m00[0:3], m10[1:2], m01[1:2])
    tiles["high"] = grads(m00[5:8], m10[6:7], m01[6:7])
    tiles["10"] = grads(m10, m00[1:-1], m11)
    tiles["01"] = grads(m01, m11, m00[1:-1])
    tiles["11"] = grads(m11, m01[2:-2], m10[2:-2])

    results = []
    for i in range(26):
        if i in (0, 19):
            results.append(jnp.where(fluid, post[i], pops[i]))
            continue
        c = VEL_ALL[i]
        lo, hi = -c[0], 3 - c[0]
        sx, sy, sz = ((1 - d) // 2 for d in c)

        def from_x():
            k, plane = crossing(0, c[0]).index(i), 5 * sx - 1
            return rx[sx, k : k + 1] + term(i, "high" if sx else "low", plane, plane)

        def t00():
            return along_x(c, post[i], from_x, from_x)

        def t10():
            k = crossing(1, c[1]).index(i)
            packed = rows(y_faces[sy], k + 2, 0) if sy else rows(y_faces[sy], k, 7)

            def edge():
                return rows(rxy[sx, sy], 4, 0) if sy else rows(rxy[sx, sy], 3, 7)

            return along_x(c, packed, edge, edge) + term(i, "10", lo, hi)

        def t01():
            k = crossing(2, c[2]).index(i)
            packed = lanes(rz[sz], k + 2, 0) if sz else lanes(rz[sz], k, 127)

            def edge():
                return lanes(rxz[sx, sz], 64, 0) if sz else lanes(rxz[sx, sz], 63, 127)

            return along_x(c, packed, edge, edge) + term(i, "01", lo, hi)

        def t11():
            packed = rows(ryz[sy][sz], 4, 0) if sy else rows(ryz[sy][sz], 3, 7)
            return packed + term(i, "11", lo, hi)

        came = shift(c, t00, t10, t01, t11)
        back = jnp.where(fluid, post[OPP_ALL[i]], pops[i])
        results.append(jnp.where(flag(i if i < 19 else i - 19), came, back))
    return results


KINDS = {
    "x": (2, 9, 8, 128),
    "y": (2, 5, 8, 128),
    "z": (2, 1, 8, 128),
    "xy": (2, 2, 1, 8, 128),
    "xz": (2, 2, 1, 8, 128),
    "yz": (2, 2, 1, 8, 128),
    "c": (2, 2, 2, 1, 128),
}


def kernel(counts, flow_hbm, phase_hbm, mask_hbm, flow_out, phase_out, *scratch):
    flow_in, phase_in, mask_in, flags, load_sem, send_sem, recv_sem = scratch[:7]
    names = list(KINDS)
    stage_refs = dict(zip(names, scratch[7:14]))
    recv_refs = dict(zip(names, scratch[14:21]))
    loads = [
        pltpu.make_async_copy(src, dst, load_sem.at[n])
        for n, (src, dst) in enumerate(
            ((phase_hbm, phase_in), (mask_hbm, mask_in), (flow_hbm, flow_in))
        )
    ]
    for load in loads:
        load.start()
    at = [lax.axis_index(a) for a in AXES]

    def exists(o):
        ok = None
        for dim, d in enumerate(o):
            if d:
                here = at[dim] > 0 if d < 0 else at[dim] < counts[dim] - 1
                ok = here if ok is None else jnp.logical_and(ok, here)
        return ok

    def peer(o):
        return tuple(at[dim] + d for dim, d in enumerate(o))

    for o in OFFS:

        @pl.when(jnp.logical_not(exists(o)))
        def _(o=o):
            for step in range(STEPS):
                ref = part({k: r.at[step] for k, r in recv_refs.items()}, o, True)
                ref[...] = jnp.zeros(ref.shape, jnp.float32)

    barrier = pltpu.get_barrier_semaphore()
    for o in OFFS:

        @pl.when(exists(o))
        def _(o=o):
            pl.semaphore_signal(barrier, inc=1, device_id=peer(o), device_id_type=MESH)

    near = 1
    for dim in range(3):
        near = near * (
            1
            + (at[dim] > 0).astype(jnp.int32)
            + (at[dim] < counts[dim] - 1).astype(jnp.int32)
        )

    def copy(step, o):
        stage = {k: r.at[step] for k, r in stage_refs.items() if k != "c"}
        recv = {k: r.at[step] for k, r in recv_refs.items()}
        first = step == 0
        if all(o):
            src = stage_refs["c"].at[step, (o[0] + 1) // 2, (o[1] + 1) // 2]
        else:
            src = part(stage, o, first)
        return pltpu.make_async_remote_copy(
            src_ref=src,
            dst_ref=part(recv, neg(o), first),
            send_sem=send_sem.at[step, SLOT[o]],
            recv_sem=recv_sem.at[step, SLOT[neg(o)]],
            device_id=peer(o),
            device_id_type=MESH,
        )

    def each(offs, action):
        for o in offs:

            @pl.when(exists(o))
            def _(o=o):
                action(o)

    faces = [o for o in OFFS if sum(map(abs, o)) == 1]
    rest = [o for o in OFFS if sum(map(abs, o)) > 1]
    for load in loads:
        load.wait()
    fluid = mask_in[...] == 1
    solid = jnp.where(fluid, 1.0, 0.0)
    pops = [flow_in[i] for i in range(19)] + [phase_in[j] for j in range(7)]
    for step in range(STEPS):
        stage = {k: r.at[step] for k, r in stage_refs.items()}
        recv = {k: r.at[step] for k, r in recv_refs.items()}
        local, _, masked = local_part(pops, fluid)
        flag_plane = solid if step == 0 else None

        def wait_recv(o, step=step, recv=recv):
            here = part(recv, o, step == 0)
            pltpu.make_async_remote_copy(
                src_ref=here,
                dst_ref=here,
                send_sem=send_sem.at[step, SLOT[o]],
                recv_sem=recv_sem.at[step, SLOT[o]],
                device_id=peer(o),
                device_id_type=MESH,
            ).wait_recv()

        def send(o, step=step):
            copy(step, o).start()

        fill_corners_and_edges(stage, local, masked, flag_plane)
        if step == 0:
            pl.semaphore_wait(barrier, near - 1)
        each(rest, send)
        fill_faces(stage, local, masked, flag_plane)
        each(faces, send)

        def wait_faces(wait_recv=wait_recv):
            each(faces, wait_recv)

        def wait_rest(wait_recv=wait_recv, step=step, recv=recv):
            each(rest, wait_recv)
            if step == 0:
                for n, value in enumerate(source_flags(recv, solid)):
                    flags[n] = jnp.where(fluid, value, 0.0)
            return lambda i: flags[i - 1] > 0.5

        pops = finish_step(recv, pops, local, masked, fluid, wait_faces, wait_rest)
    for i in range(19):
        flow_out[i] = pops[i]
    for j in range(7):
        phase_out[j] = pops[19 + j]
    for step in range(STEPS):
        for o in OFFS:

            @pl.when(exists(o))
            def _(o=o, step=step):
                copy(step, o).wait_send()


def drain(flow_in, phase_in, flow_out, phase_out, sems):
    copies = [
        pltpu.make_async_copy(flow_in, flow_out, sems.at[0]),
        pltpu.make_async_copy(phase_in, phase_out, sems.at[1]),
    ]
    for copy in copies:
        copy.start()
    for copy in copies:
        copy.wait()


def solution(mesh):
    counts = [mesh.shape[a] for a in AXES]

    def shards(flow_pops, phase_pops, pore_mask):
        f32 = jnp.float32
        stage_kinds = dict(KINDS, c=(2, 2, 1, 128))
        shapes = (
            jax.ShapeDtypeStruct(flow_pops.shape, f32),
            jax.ShapeDtypeStruct(phase_pops.shape, f32),
        )
        vmem, hbm = pl.BlockSpec(memory_space=pltpu.VMEM), pl.BlockSpec(memory_space=pltpu.HBM)
        results = pl.pallas_call(
            lambda *refs: kernel(counts, *refs),
            out_shape=shapes,
            in_specs=[hbm] * 3,
            out_specs=(vmem, vmem),
            scratch_shapes=[
                pltpu.VMEM((19, 4, 8, 128), f32),
                pltpu.VMEM((7, 4, 8, 128), f32),
                pltpu.VMEM((4, 8, 128), jnp.int32),
                pltpu.VMEM((18, 4, 8, 128), f32),
                pltpu.SemaphoreType.DMA((3,)),
                pltpu.SemaphoreType.DMA((STEPS, 26)),
                pltpu.SemaphoreType.DMA((STEPS, 26)),
            ]
            + [pltpu.VMEM((STEPS, *shape), f32) for shape in stage_kinds.values()]
            + [pltpu.VMEM((STEPS, *shape), f32) for shape in KINDS.values()],
            compiler_params=pltpu.CompilerParams(
                collective_id=0, has_side_effects=True, vmem_limit_bytes=32 << 20
            ),
            name="lattice_steps",
        )(*(pltpu.with_memory_space_constraint(v, pltpu.HBM) for v in (flow_pops, phase_pops, pore_mask)))
        return pl.pallas_call(
            drain,
            out_shape=shapes,
            in_specs=[vmem, vmem],
            out_specs=(hbm, hbm),
            scratch_shapes=[pltpu.SemaphoreType.DMA((2,))],
            name="drain",
        )(*(pltpu.with_memory_space_constraint(v, pltpu.VMEM) for v in results))

    return jax.shard_map(
        shards,
        mesh=mesh,
        in_specs=(P(None, *AXES), P(None, *AXES), P(*AXES)),
        out_specs=(P(None, *AXES), P(None, *AXES)),
        check_vma=False,
    )
```

```python
import itertools

import jax
import jax.numpy as jnp
from jax import lax
from jax.experimental import pallas as pl
from jax.experimental.pallas import tpu as pltpu
from jax.sharding import PartitionSpec as P

MESH = pl.DeviceIdType.MESH
AXES = ("gx", "gy", "gz")
VEL = [
    (0, 0, 0),
    (1, 0, 0),
    (-1, 0, 0),
    (0, 1, 0),
    (0, -1, 0),
    (0, 0, 1),
    (0, 0, -1),
    (1, 1, 0),
    (-1, -1, 0),
    (1, -1, 0),
    (-1, 1, 0),
    (1, 0, 1),
    (-1, 0, -1),
    (1, 0, -1),
    (-1, 0, 1),
    (0, 1, 1),
    (0, -1, -1),
    (0, 1, -1),
    (0, -1, 1),
]
INDEX = {c: i for i, c in enumerate(VEL)}
OPP = [0, 2, 1, 4, 3, 6, 5, 8, 7, 10, 9, 12, 11, 14, 13, 16, 15, 18, 17]
VEL_ALL = VEL + VEL[:7]
OPP_ALL = OPP + [19 + j for j in OPP[:7]]
WT = [1.0 / 3.0] + [1.0 / 18.0] * 6 + [1.0 / 36.0] * 12
BT = [-2.0 / 9.0] + [1.0 / 54.0] * 6 + [1.0 / 27.0] * 12
OFFS = sorted(
    (o for o in itertools.product((-1, 0, 1), repeat=3) if any(o)),
    key=lambda o: -sum(map(abs, o)),
)
SLOT = {o: n for n, o in enumerate(OFFS)}


PLUS = [i for i in range(19) if VEL[i][0] > 0]
MINUS = [i for i in range(19) if VEL[i][0] < 0]
LEVEL = [i for i in range(19) if VEL[i][0] == 0]
ORDER = PLUS + [19, 22, 23, 24, 25, 20, "masked", "solid", 21] + MINUS + LEVEL
FIELD = {name: k for k, name in enumerate(ORDER)}
MASKED, SOLID = FIELD["masked"], FIELD["solid"]
FLIP_Y = {"00": "10", "10": "00", "01": "11", "11": "01"}
FLIP_Z = {"00": "01", "01": "00", "10": "11", "11": "10"}


def neg(o):
    return tuple(-d for d in o)


def iota(dim):
    return lax.broadcasted_iota(jnp.int32, (1, 8, 128), dim)


def roll(v, shift, axis):
    size = v.shape[axis]
    shift %= size
    return pltpu.roll(v, shift, axis) if shift else v


def sel(mask, a, b):
    return jnp.where(jnp.broadcast_to(mask, a.shape), a, b)


def local_part(pops, fluid):
    f, g = pops[:19], pops[19:]
    phase = ((g[0] + g[1]) + (g[2] + g[3])) + ((g[4] + g[5]) + g[6])
    masked = jnp.where(fluid, phase, 0.0)
    sums = {i: f[i] + f[OPP[i]] for i in range(1, 19, 2)}
    diff = {i: f[i] - f[OPP[i]] for i in range(1, 19, 2)}
    density = f[0]
    for i in range(1, 19, 2):
        density = density + sums[i]
    inv = 1.0 / density
    mom = []
    for dim in range(3):
        total = None
        for i in range(1, 19, 2):
            s = VEL[i][dim]
            if s:
                term = diff[i]
                total = term if total is None else (total + term if s > 0 else total - term)
        mom.append(total)
    flow = [m * inv for m in mom]
    speed_sq = flow[0] * flow[0] + flow[1] * flow[1] + flow[2] * flow[2]
    omega = 1.0 / (0.8 + 0.2 * phase)
    keep = 1.0 - omega
    base = omega * density
    even0 = base * (1.0 - 1.5 * speed_sq)
    out = [None] * 26
    out[0] = keep * f[0] + WT[0] * even0
    for i in range(1, 19, 2):
        c = VEL[i]
        along = None
        for dim in range(3):
            if c[dim]:
                term = flow[dim]
                along = term if along is None else (along + term if c[dim] > 0 else along - term)
        even = WT[i] * even0 + (4.5 * WT[i]) * base * (along * along)
        odd = (3.0 * WT[i]) * base * along
        out[i] = keep * f[i] + (even + odd)
        out[i + 1] = keep * f[i + 1] + (even - odd)
    out[19] = (1.25 * 0.25) * phase - 0.25 * g[0]
    eighth = (1.25 * 0.125) * phase
    for dim in range(3):
        odd = 4.0 * eighth * flow[dim]
        out[20 + 2 * dim] = (eighth + odd) - 0.25 * g[1 + 2 * dim]
        out[21 + 2 * dim] = (eighth - odd) - 0.25 * g[2 + 2 * dim]
    return out, phase, masked


def pair_shift(own, halo, sign, axis):
    size = own.shape[axis]
    at = iota(axis)
    if sign > 0:
        return sel(at == 0, roll(halo, 1, axis), roll(own, 1, axis))
    return sel(at == size - 1, roll(halo, -1, axis), roll(own, -1, axis))


def join(*parts):
    return jnp.concatenate(parts, axis=0)


def minus_plus(minus, plus, axis):
    half = 4 if axis == 1 else 64
    return sel(iota(axis) < half, plus, minus)


def pieces(o):
    dx, dy, dz = o

    def planes(near, far):
        here = 8 - far if dx > 0 else 3 + near
        return pl.ds(here, far - near + 1), pl.ds(here + (-4 if dx > 0 else 4), far - near + 1)

    def lines(depth):
        return pl.ds(8 - depth, depth) if dy > 0 else pl.ds(0, depth)

    every, mid = pl.ds(0, 8), pl.ds(4, 4)
    flow = (pl.ds(0, 5), pl.ds(14, 14))
    if dz:
        here, there = (pl.ds(0, 4), planes(1, 4)[1]) if dx else (pl.ds(0, 4), mid)
        side = pl.ds((1 - dz) // 2, 1)
        row = lines(4) if dy else every
        return [("z1" if dy else "z0", (pl.ds((1 + dz) // 2, 1), here, row), (side, there, row))]
    out = []

    def add(name, fields, where, row):
        out.append((name, (fields, where[0], row), (fields, where[1], row)))

    if dx and not dy:
        add("e0", pl.ds(0, 28), planes(1, 1), every)
        add("e0", pl.ds(0 if dx > 0 else 5, 14), planes(2, 2), every)
        add("e0", pl.ds(10 if dx > 0 else 11, 3), planes(3, 4), every)
    elif dx:
        for fields in flow:
            add("e1", fields, planes(1, 2), lines(2))
        add("e1", pl.ds(5, 9), planes(1, 2), lines(4))
        add("e1", pl.ds(5, 9), planes(3, 4), lines(2))
    else:
        for fields in flow:
            add("e1", fields, (mid, mid), lines(2))
        add("e1", pl.ds(5, 9), (mid, mid), lines(4))
    return out


def exchange(counts, flow_hbm, phase_hbm, mask_hbm, flow_in, phase_in, e0, e1, z0, z1, *scratch):
    mask_in, packed, load_sem, send_sem, recv_sem = scratch
    loads = [
        pltpu.make_async_copy(src, dst, load_sem.at[n])
        for n, (src, dst) in enumerate(
            ((phase_hbm, phase_in), (mask_hbm, mask_in), (flow_hbm, flow_in))
        )
    ]
    for load in loads:
        load.start()
    at = [lax.axis_index(a) for a in AXES]

    def exists(o):
        ok = None
        for dim, d in enumerate(o):
            if d:
                here = at[dim] > 0 if d < 0 else at[dim] < counts[dim] - 1
                ok = here if ok is None else jnp.logical_and(ok, here)
        return ok

    def peer(o):
        return tuple(at[dim] + d for dim, d in enumerate(o))

    for o in OFFS:

        @pl.when(jnp.logical_not(exists(o)))
        def _(o=o):
            dx, dy, dz = o
            planes = slice(0, 4) if dx < 0 else slice(8, 12) if dx else slice(4, 8)
            row = slice(4, 8) if dy < 0 else slice(0, 4) if dy else slice(0, 8)
            zeros = jnp.zeros((2, 4, 4 if dy else 8, 128), jnp.float32)
            if dz:
                (z1 if dy else z0)[(1 + dz) // 2, planes, row] = zeros[0]
            else:
                (e1 if dy else e0)[MASKED : SOLID + 1, planes, row] = zeros

    barrier = pltpu.get_barrier_semaphore()
    for o in OFFS:

        @pl.when(exists(o))
        def _(o=o):
            pl.semaphore_signal(barrier, inc=1, device_id=peer(o), device_id_type=MESH)

    near = 1
    for dim in range(3):
        near = near * (
            1
            + (at[dim] > 0).astype(jnp.int32)
            + (at[dim] < counts[dim] - 1).astype(jnp.int32)
        )
    arrays = {"e0": e0, "e1": e1, "z0": z0, "z1": z1}

    def copies(o):
        for n, (name, here, there) in enumerate(pieces(o)):
            src = packed if name[0] == "z" else e0
            yield pltpu.make_async_remote_copy(
                src_ref=src.at[here],
                dst_ref=arrays[name].at[there],
                send_sem=send_sem.at[SLOT[o], n],
                recv_sem=recv_sem.at[SLOT[neg(o)], n],
                device_id=peer(o),
                device_id_type=MESH,
            )

    for load in loads:
        load.wait()
    fluid = mask_in[...] == 1
    pops = [flow_in[i] for i in range(19)] + [phase_in[j] for j in range(7)]
    values, _, masked = local_part(pops, fluid)
    values = dict(enumerate(values), masked=masked, solid=jnp.where(fluid, 1.0, 0.0))
    lane = iota(2)
    blocks = [None, None]
    for k, name in enumerate(ORDER):
        v = values[name]
        e0[k, 4:8] = v
        for side in (0, 1):
            moved = roll(v, 4 * k + 4 * side, 2)
            blocks[side] = moved if k == 0 else sel(lane >= 4 * k, moved, blocks[side])
    for side in (0, 1):
        packed[side] = blocks[side]
    pl.semaphore_wait(barrier, near - 1)
    for o in OFFS:

        @pl.when(exists(o))
        def _(o=o):
            for copy in copies(o):
                copy.start()

    for o in OFFS:

        @pl.when(exists(o))
        def _(o=o):
            for n, (name, _, there) in enumerate(pieces(neg(o))):
                ref = arrays[name].at[there]
                pltpu.make_async_remote_copy(
                    src_ref=ref,
                    dst_ref=ref,
                    send_sem=send_sem.at[SLOT[o], n],
                    recv_sem=recv_sem.at[SLOT[o], n],
                    device_id=peer(o),
                    device_id_type=MESH,
                ).wait_recv()

    for o in OFFS:

        @pl.when(exists(o))
        def _(o=o):
            for copy in copies(o):
                copy.wait_send()


def cut(ranged, lo, hi):
    v, first = ranged
    return v[lo - first : hi - first + 1]


class Step:
    def __init__(self, masked, local, grad_range, flow_range, phase_range):
        self.local, self.flow_range, self.phase_range = local, flow_range, phase_range
        self.known, self.grads = {}, {}
        for tile, (lo, hi) in grad_range.items():
            wide, mid = cut(masked[tile], lo - 1, hi + 1), cut(masked[tile], lo, hi)
            in_y, in_z = (cut(masked[flip[tile]], lo, hi) for flip in (FLIP_Y, FLIP_Z))
            gx = 0.5 * (wide[2:] - wide[:-2])
            gy = 0.5 * (pair_shift(mid, in_y, -1, 1) - pair_shift(mid, in_y, 1, 1))
            gz = 0.5 * (pair_shift(mid, in_z, -1, 2) - pair_shift(mid, in_z, 1, 2))
            square = gx * gx + gy * gy + gz * gz + 0.01
            inv = lax.rsqrt(square)
            self.grads[tile] = tuple((v, lo) for v in (gx, gy, gz, inv, square * inv, mid))

    def term(self, i, tile):
        if i == 0:
            lo, hi = self.flow_range(tile, 0)
            return -(0.5 * BT[0]) * cut(self.grads[tile][4], lo, hi), lo
        odd = i - 1 if i < 19 else i - 20
        pair = i - odd % 2
        key = (pair, tile)
        c = VEL_ALL[pair]
        lo, hi = (self.flow_range if i < 19 else self.phase_range)(tile, c[0])
        if key not in self.known:
            g = [cut(v, lo, hi) for v in self.grads[tile]]
            cross = None
            for dim in range(3):
                if c[dim]:
                    cross = g[dim] if cross is None else (cross + g[dim] if c[dim] > 0 else cross - g[dim])
            if i < 19:
                v = (0.5 * WT[pair]) * (cross * cross * g[3]) - (0.5 * BT[pair]) * g[4]
            else:
                v = (0.875 * 0.125) * ((1.0 - g[5] * g[5]) * (cross * g[3]))
            self.known[key] = v
        v = self.known[key]
        return (-v if i >= 19 and odd % 2 else v), lo

    def post(self, i, tile, lo, hi):
        key = ("post", i, tile, lo, hi)
        if key not in self.known:
            v = cut(self.local(i, tile), lo, hi)
            self.known[key] = v if i == 19 else v + cut(self.term(i, tile), lo, hi)
        return self.known[key]


def moved(read, c, tile, lo, hi):
    lo, hi = lo - c[0], hi - c[0]

    def in_y(name):
        v = read(name, lo, hi)
        return pair_shift(v, read(FLIP_Y[name], lo, hi), c[1], 1) if c[1] else v

    v = in_y(tile)
    return pair_shift(v, in_y(FLIP_Z[tile]), c[2], 2) if c[2] else v


def two_steps(flow_in, phase_in, e0, e1, z0, z1, flow_out, phase_out, buf, sems):
    fields = {}

    def field(k, tile):
        if (k, tile) not in fields:
            if tile[1] == "0":
                v = (e1 if tile == "10" else e0)[k]
            else:
                z = z1 if tile == "11" else z0
                v = minus_plus(roll(z[0], -(4 * k + 4), 2), roll(z[1], -4 * k, 2), 2)
            fields[k, tile] = (v, -4)
        return fields[k, tile]

    tiles = ("00", "10", "01", "11")
    first = Step(
        {t: field(MASKED, t) for t in tiles},
        lambda i, t: field(FIELD[i], t),
        {t: (-2, 5) if t == "11" else (-3, 6) for t in tiles},
        lambda t, cx: (-2, 5) if cx else (-1, 4),
        lambda t, cx: (-3, 6) if cx and t != "11" else (-2, 5),
    )
    flow_planes = {"00": (-1, 4), "10": (-1, 4), "01": (-1, 4), "11": (0, 3)}
    phase_planes = {"00": (-2, 5), "10": (-2, 5), "01": (-2, 5), "11": (-1, 4)}
    flags = {}

    def flag(c, tile, lo, hi):
        key = (c, tile)
        if key not in flags:
            axis = sum(map(abs, c)) == 1
            first_plane, last = (phase_planes if axis else flow_planes)[tile]
            flags[key] = (
                moved(lambda t, a, b: cut(field(SOLID, t), a, b), c, tile, first_plane, last),
                first_plane,
            )
        return cut(flags[key], lo, hi) > 0.5

    def propagated(step, i, tile, lo, hi):
        if i in (0, 19):
            return step.post(i, tile, lo, hi)
        c = VEL_ALL[i]
        came = moved(lambda t, a, b: step.post(i, t, a, b), c, tile, lo, hi)
        return jnp.where(flag(c, tile, lo, hi), came, step.post(OPP_ALL[i], tile, lo, hi))

    masked, later = {}, {}
    for tile in tiles:
        lo, hi = phase_planes[tile]
        phases = [propagated(first, 19 + j, tile, lo, hi) for j in range(7)]
        total = phases[0]
        for v in phases[1:]:
            total = total + v
        masked[tile] = (jnp.where(cut(field(SOLID, tile), lo, hi) > 0.5, total, 0.0), lo)
        a, b = flow_planes[tile]
        pops = [propagated(first, i, tile, a, b) for i in range(19)]
        pops += [cut((v, lo), a, b) for v in phases]
        values, _, _ = local_part(pops, cut(field(SOLID, tile), a, b) > 0.5)
        for i, v in enumerate(values):
            later[i, tile] = (v, a)
    second = Step(
        masked,
        lambda i, t: later[i, t],
        {t: flow_planes[t] for t in tiles},
        lambda t, cx: (-1, 4) if cx else (0, 3),
        lambda t, cx: (-1, 4) if cx else (0, 3),
    )
    fluid = e0[SOLID, 4:8] > 0.5
    copies = []
    for i in range(26):
        raw = flow_in[i] if i < 19 else phase_in[i - 19]
        buf[i] = jnp.where(fluid, propagated(second, i, "00", 0, 3), raw)
        out = flow_out.at[i] if i < 19 else phase_out.at[i - 19]
        copies.append(pltpu.make_async_copy(buf.at[i], out, sems.at[i]))
        copies[-1].start()
    for copy in copies:
        copy.wait()


def solution(mesh):
    counts = [mesh.shape[a] for a in AXES]

    def shards(flow_pops, phase_pops, pore_mask):
        f32 = jnp.float32
        shapes = tuple(jax.ShapeDtypeStruct(v.shape, f32) for v in (flow_pops, phase_pops))
        halo = tuple(
            jax.ShapeDtypeStruct(shape, f32)
            for shape in [(28, 12, 8, 128)] * 2 + [(2, 12, 8, 128)] * 2
        )
        vmem, hbm = pl.BlockSpec(memory_space=pltpu.VMEM), pl.BlockSpec(memory_space=pltpu.HBM)
        near = pl.pallas_call(
            lambda *refs: exchange(counts, *refs),
            out_shape=shapes + halo,
            in_specs=[hbm] * 3,
            out_specs=(vmem,) * 6,
            scratch_shapes=[
                pltpu.VMEM((4, 8, 128), jnp.int32),
                pltpu.VMEM((2, 4, 8, 128), f32),
                pltpu.SemaphoreType.DMA((3,)),
                pltpu.SemaphoreType.DMA((26, 4)),
                pltpu.SemaphoreType.DMA((26, 4)),
            ],
            compiler_params=pltpu.CompilerParams(
                collective_id=0, has_side_effects=True, vmem_limit_bytes=24 << 20
            ),
            name="exchange",
        )(*(pltpu.with_memory_space_constraint(v, pltpu.HBM) for v in (flow_pops, phase_pops, pore_mask)))
        return pl.pallas_call(
            two_steps,
            out_shape=shapes,
            in_specs=[vmem] * 6,
            out_specs=(hbm, hbm),
            scratch_shapes=[pltpu.VMEM((26, 4, 8, 128), f32), pltpu.SemaphoreType.DMA((26,))],
            compiler_params=pltpu.CompilerParams(vmem_limit_bytes=40 << 20),
            name="two_steps",
        )(*(pltpu.with_memory_space_constraint(v, pltpu.VMEM) for v in near))

    return jax.shard_map(
        shards,
        mesh=mesh,
        in_specs=(P(None, *AXES), P(None, *AXES), P(*AXES)),
        out_specs=(P(None, *AXES), P(None, *AXES)),
        check_vma=False,
    )
```

```python
import itertools

import jax
import jax.numpy as jnp
from jax import lax
from jax.experimental import pallas as pl
from jax.experimental.pallas import tpu as pltpu
from jax.sharding import PartitionSpec as P

STEPS = 2
MESH = pl.DeviceIdType.MESH
AXES = ("gx", "gy", "gz")
VEL = [
    (0, 0, 0),
    (1, 0, 0),
    (-1, 0, 0),
    (0, 1, 0),
    (0, -1, 0),
    (0, 0, 1),
    (0, 0, -1),
    (1, 1, 0),
    (-1, -1, 0),
    (1, -1, 0),
    (-1, 1, 0),
    (1, 0, 1),
    (-1, 0, -1),
    (1, 0, -1),
    (-1, 0, 1),
    (0, 1, 1),
    (0, -1, -1),
    (0, 1, -1),
    (0, -1, 1),
]
INDEX = {c: i for i, c in enumerate(VEL)}
OPP = [0, 2, 1, 4, 3, 6, 5, 8, 7, 10, 9, 12, 11, 14, 13, 16, 15, 18, 17]
VEL_ALL = VEL + VEL[:7]
OPP_ALL = OPP + [19 + j for j in OPP[:7]]
WT = [1.0 / 3.0] + [1.0 / 18.0] * 6 + [1.0 / 36.0] * 12
BT = [-2.0 / 9.0] + [1.0 / 54.0] * 6 + [1.0 / 27.0] * 12
OFFS = sorted(
    (o for o in itertools.product((-1, 0, 1), repeat=3) if any(o)),
    key=lambda o: (-sum(map(abs, o)), o[1] == 0, o[2] != 0),
)
SLOT = {o: n for n, o in enumerate(OFFS)}


def neg(o):
    return tuple(-d for d in o)


def crossing(dim, sign):
    flow = [i for i in range(19) if VEL[i][dim] == sign]
    return flow + [19 + INDEX[tuple(sign if d == dim else 0 for d in range(3))]]


def iota(dim):
    return lax.broadcasted_iota(jnp.int32, (1, 8, 128), dim)


def roll(v, shift, axis):
    size = v.shape[axis]
    shift %= size
    return pltpu.roll(v, shift, axis) if shift else v


def rows(v, frm, to):
    return roll(v, to - frm, 1)


def lanes(v, frm, to):
    return roll(v, to - frm, 2)


def sel(mask, a, b):
    return jnp.where(jnp.broadcast_to(mask, a.shape), a, b)


def local_part(pops, fluid):
    f, g = pops[:19], pops[19:]
    phase = ((g[0] + g[1]) + (g[2] + g[3])) + ((g[4] + g[5]) + g[6])
    masked = jnp.where(fluid, phase, 0.0)
    sums = {i: f[i] + f[OPP[i]] for i in range(1, 19, 2)}
    diff = {i: f[i] - f[OPP[i]] for i in range(1, 19, 2)}
    density = f[0]
    for i in range(1, 19, 2):
        density = density + sums[i]
    inv = 1.0 / density
    mom = []
    for dim in range(3):
        total = None
        for i in range(1, 19, 2):
            s = VEL[i][dim]
            if s:
                term = diff[i]
                total = term if total is None else (total + term if s > 0 else total - term)
        mom.append(total)
    flow = [m * inv for m in mom]
    speed_sq = flow[0] * flow[0] + flow[1] * flow[1] + flow[2] * flow[2]
    omega = 1.0 / (0.8 + 0.2 * phase)
    keep = 1.0 - omega
    base = omega * density
    even0 = base * (1.0 - 1.5 * speed_sq)
    out = [None] * 26
    out[0] = keep * f[0] + WT[0] * even0
    for i in range(1, 19, 2):
        c = VEL[i]
        along = None
        for dim in range(3):
            if c[dim]:
                term = flow[dim]
                along = term if along is None else (along + term if c[dim] > 0 else along - term)
        even = WT[i] * even0 + (4.5 * WT[i]) * base * (along * along)
        odd = (3.0 * WT[i]) * base * along
        out[i] = keep * f[i] + (even + odd)
        out[i + 1] = keep * f[i + 1] + (even - odd)
    out[19] = (1.25 * 0.25) * phase - 0.25 * g[0]
    eighth = (1.25 * 0.125) * phase
    for dim in range(3):
        odd = 4.0 * eighth * flow[dim]
        out[20 + 2 * dim] = (eighth + odd) - 0.25 * g[1 + 2 * dim]
        out[21 + 2 * dim] = (eighth - odd) - 0.25 * g[2 + 2 * dim]
    return out, phase, masked


def merge_planes(v, block, offset):
    lane = iota(2)
    acc = roll(v[0:1], offset, 2)
    for x in range(1, 4):
        acc = sel(lane >= block * x, roll(v[x : x + 1], block * x + offset, 2), acc)
    return acc


def split_planes(v, block, offset):
    return join(*(roll(v, -(block * x + offset), 2) for x in range(4)))


def fill_corners_and_edges(stage, local, masked, solid):
    row, lane = iota(1), iota(2)
    for sa, sb in itertools.product((0, 1), repeat=2):
        near, far = (3, 2) if sa else (0, 1)
        xs, fs = slice(near, near + 1), slice(far, far + 1)
        ga, gb = 2 * sa - 1, 2 * sb - 1
        edge = 7 if sb else 0
        stage["c"][sa, sb] = masked[near][edge : edge + 1]
        acc = masked
        edge, pop, flag = (7, 3, 2) if sa else (0, 4, 5)
        acc = sel(row == pop, rows(local[INDEX[(0, ga, gb)]], edge, pop), acc)
        if solid is not None:
            acc = sel(row == flag, rows(solid, edge, flag), acc)
        stage["yz"][sa, sb] = merge_planes(acc, 2, 2 * sb)
        acc = masked[xs]
        edge, pop, flag, deep = (127, 63, 62, 61) if sb else (0, 64, 65, 66)
        acc = sel(lane == pop, lanes(local[INDEX[(ga, 0, gb)]][xs], edge, pop), acc)
        acc = sel(lane == deep, lanes(masked[fs], edge, deep), acc)
        if solid is not None:
            acc = sel(lane == flag, lanes(solid[xs], edge, flag), acc)
        stage["xz"][sa, sb] = acc
        acc = masked[xs]
        edge, pop, flag, deep = (7, 3, 2, 4) if sb else (0, 4, 5, 3)
        acc = sel(row == pop, rows(local[INDEX[(ga, gb, 0)]][xs], edge, pop), acc)
        acc = sel(row == deep, rows(masked[fs], edge, deep), acc)
        if solid is not None:
            acc = sel(row == flag, rows(solid[xs], edge, flag), acc)
        stage["xy"][sa, sb] = acc


def fill_faces(stage, local, masked, solid):
    row, lane = iota(1), iota(2)
    for side, sign in ((0, -1), (1, 1)):
        near, far = (3, 2) if side else (0, 1)
        acc = masked
        edge, first = (127, 0) if side else (0, 2)
        for k, i in enumerate(crossing(2, sign)):
            acc = sel(lane == first + k, lanes(local[i], edge, first + k), acc)
        if solid is not None:
            acc = sel(lane == first + 6, lanes(solid, edge, first + 6), acc)
        stage["z"][side] = merge_planes(acc, 16, 2 * side)
        acc = masked
        edge, first = (7, 0) if side else (0, 2)
        for k, i in enumerate(crossing(1, sign)):
            acc = sel(row == first + k, rows(local[i], edge, first + k), acc)
        stage["y"][side, 0:4] = acc
        if solid is not None:
            acc = rows(solid[0:1], edge, 0)
            for x in range(1, 4):
                acc = sel(row == x, rows(solid[x : x + 1], edge, x), acc)
            stage["y"][side, 4:5] = acc
        out = stage["x"]
        for k, i in enumerate(crossing(0, sign)):
            out[side, k] = local[i][near]
        out[side, 6] = masked[near]
        out[side, 7] = masked[far]
        if solid is not None:
            out[side, 8] = solid[near]


def part(bufs, o, first):
    a, b, c = ((d + 1) // 2 for d in o)
    kind = tuple(d != 0 for d in o)
    if kind == (True, False, False):
        return bufs["x"].at[a, pl.ds(0, 9 if first else 8)]
    if kind == (False, True, False):
        return bufs["y"].at[b, pl.ds(0, 5 if first else 4)]
    if kind == (False, False, True):
        return bufs["z"].at[c]
    if kind == (True, True, False):
        return bufs["xy"].at[a, b]
    if kind == (True, False, True):
        return bufs["xz"].at[a, c]
    if kind == (False, True, True):
        return bufs["yz"].at[b, c]
    return bufs["c"].at[a, b, c]


def pair_shift(own, halo, sign, axis):
    size = own.shape[axis]
    at = iota(axis)
    if sign > 0:
        return sel(at == 0, roll(halo, 1, axis), roll(own, 1, axis))
    return sel(at == size - 1, roll(halo, -1, axis), roll(own, -1, axis))


def shift(c, t00, t10, t01, t11):
    if c[1]:
        t00 = pair_shift(t00(), t10(), c[1], 1)
        halo = (lambda: pair_shift(t01(), t11(), c[1], 1)) if c[2] else None
    else:
        t00, halo = t00(), t01
    return pair_shift(t00, halo(), c[2], 2) if c[2] else t00


def join(*parts):
    return jnp.concatenate(parts, axis=0)


def minus_plus(minus, plus, axis):
    at = iota(axis)
    half = 4 if axis == 1 else 64
    return sel(at < half, plus, minus)


def along_x(c, own, low, high):
    if c[0] > 0:
        return join(low(), own[0:3])
    if c[0] < 0:
        return join(own[1:4], high())
    return own


def source_flags(recv, solid):
    y = [recv["y"][s, 4:5] for s in (0, 1)]
    y = join(*(minus_plus(rows(y[0], x, 7), rows(y[1], x, 0), 1) for x in range(4)))
    z = [split_planes(recv["z"][s], 16, 2 * (1 - s)) for s in (0, 1)]
    z = minus_plus(lanes(z[0], 6, 127), lanes(z[1], 8, 0), 2)
    x = [recv["x"][s, 8:9] for s in (0, 1)]
    xy = [
        minus_plus(rows(recv["xy"][s, 0], 2, 7), rows(recv["xy"][s, 1], 5, 0), 1) for s in (0, 1)
    ]
    xz = [
        minus_plus(lanes(recv["xz"][s, 0], 62, 127), lanes(recv["xz"][s, 1], 65, 0), 2)
        for s in (0, 1)
    ]
    yz = [
        minus_plus(rows(recv["yz"][0, s], 2, 7), rows(recv["yz"][1, s], 5, 0), 1) for s in (0, 1)
    ]
    yz = [split_planes(yz[s], 2, 2 * (1 - s)) for s in (0, 1)]
    yz = minus_plus(yz[0], yz[1], 2)
    flags = []
    for i in range(1, 19):
        c = VEL[i]
        flags.append(
            shift(
                c,
                lambda: along_x(c, solid, lambda: x[0], lambda: x[1]),
                lambda: along_x(c, y, lambda: xy[0], lambda: xy[1]),
                lambda: along_x(c, z, lambda: xz[0], lambda: xz[1]),
                lambda: yz,
            )
        )
    return flags


def finish_step(recv, pops, local, masked, fluid, wait_faces, wait_rest):
    def grads(own, in_y, in_z):
        mid = own[1:-1]
        gx = 0.5 * (own[2:] - own[:-2])
        gy = 0.5 * (pair_shift(mid, in_y, -1, 1) - pair_shift(mid, in_y, 1, 1))
        gz = 0.5 * (pair_shift(mid, in_z, -1, 2) - pair_shift(mid, in_z, 1, 2))
        square = gx * gx + gy * gy + gz * gz + 0.01
        inv = lax.rsqrt(square)
        return ((gx, gy, gz), inv, square * inv, mid)

    tiles, known = {}, {}
    first_plane = {"00": 0, "low": -1, "high": 4, "10": -1, "01": -1, "11": 0}

    def cut(v, name, lo, hi):
        base = first_plane[name]
        return v[lo - base : hi - base + 1]

    def term(i, name, lo, hi):
        grad, inv, mag, phase = tiles[name]
        if i >= 19:
            dim, sign = (i - 20) // 2, 1 - 2 * ((i - 20) % 2)
            key = ("g", dim, name, lo, hi)
            if key not in known:
                p, d, r = (cut(v, name, lo, hi) for v in (phase, grad[dim], inv))
                known[key] = (0.875 * 0.125) * ((1.0 - p * p) * (d * r))
            return known[key] if sign > 0 else -known[key]
        pair = i if i % 2 else i - 1
        key = (pair, name, lo, hi)
        if key not in known:
            cross = None
            for dim in range(3):
                if VEL[pair][dim]:
                    d = cut(grad[dim], name, lo, hi)
                    cross = (
                        d if cross is None else (cross + d if VEL[pair][dim] > 0 else cross - d)
                    )
            r, m = cut(inv, name, lo, hi), cut(mag, name, lo, hi)
            known[key] = (0.5 * WT[pair]) * (cross * cross * r) - (0.5 * BT[pair]) * m
        return known[key]

    wait_faces()
    rx, ry = recv["x"], recv["y"]
    rz = [split_planes(recv["z"][s], 16, 2 * (1 - s)) for s in (0, 1)]
    y_faces = [ry[s, 0:4] for s in (0, 1)]
    m00 = join(rx[0, 7:8], rx[0, 6:7], masked, rx[1, 6:7], rx[1, 7:8])
    m10 = minus_plus(y_faces[0], y_faces[1], 1)
    m01 = minus_plus(rz[0], rz[1], 2)
    tiles["00"] = grads(m00[1:-1], m10, m01)
    post = [None] * 26
    post[0] = local[0] - (0.5 * BT[0]) * tiles["00"][2]
    post[19] = local[19]
    for i in itertools.chain(range(1, 19), range(20, 26)):
        post[i] = local[i] + term(i, "00", 0, 3)

    flag = wait_rest()
    rxy, rxz, rc = recv["xy"], recv["xz"], recv["c"]
    ryz = [[split_planes(recv["yz"][b, c], 2, 2 * (1 - c)) for c in (0, 1)] for b in (0, 1)]

    def deep_xy(s):
        return minus_plus(rows(rxy[s, 0], 4, 7), rows(rxy[s, 1], 3, 0), 1)

    def deep_xz(s):
        return minus_plus(lanes(rxz[s, 0], 61, 127), lanes(rxz[s, 1], 66, 0), 2)

    def near_xy(s):
        return minus_plus(rxy[s, 0], rxy[s, 1], 1)

    def near_xz(s):
        return minus_plus(rxz[s, 0], rxz[s, 1], 2)

    def corner(s):
        line = [[jnp.broadcast_to(rc[s, b, c][None], (1, 8, 128)) for c in (0, 1)] for b in (0, 1)]
        return minus_plus(minus_plus(*line[0], 2), minus_plus(*line[1], 2), 1)

    m10 = join(deep_xy(0), near_xy(0), m10, near_xy(1), deep_xy(1))
    m01 = join(deep_xz(0), near_xz(0), m01, near_xz(1), deep_xz(1))
    m11 = join(
        corner(0), minus_plus(minus_plus(*ryz[0], 2), minus_plus(*ryz[1], 2), 1), corner(1)
    )
    tiles["low"] = grads(m00[0:3], m10[1:2], m01[1:2])
    tiles["high"] = grads(m00[5:8], m10[6:7], m01[6:7])
    tiles["10"] = grads(m10, m00[1:-1], m11)
    tiles["01"] = grads(m01, m11, m00[1:-1])
    tiles["11"] = grads(m11, m01[2:-2], m10[2:-2])

    results = []
    for i in range(26):
        if i in (0, 19):
            results.append(jnp.where(fluid, post[i], pops[i]))
            continue
        c = VEL_ALL[i]
        lo, hi = -c[0], 3 - c[0]
        sx, sy, sz = ((1 - d) // 2 for d in c)

        def from_x():
            k, plane = crossing(0, c[0]).index(i), 5 * sx - 1
            return rx[sx, k : k + 1] + term(i, "high" if sx else "low", plane, plane)

        def t00():
            return along_x(c, post[i], from_x, from_x)

        def t10():
            k = crossing(1, c[1]).index(i)
            packed = rows(y_faces[sy], k + 2, 0) if sy else rows(y_faces[sy], k, 7)

            def edge():
                return rows(rxy[sx, sy], 4, 0) if sy else rows(rxy[sx, sy], 3, 7)

            return along_x(c, packed, edge, edge) + term(i, "10", lo, hi)

        def t01():
            k = crossing(2, c[2]).index(i)
            packed = lanes(rz[sz], k + 2, 0) if sz else lanes(rz[sz], k, 127)

            def edge():
                return lanes(rxz[sx, sz], 64, 0) if sz else lanes(rxz[sx, sz], 63, 127)

            return along_x(c, packed, edge, edge) + term(i, "01", lo, hi)

        def t11():
            packed = rows(ryz[sy][sz], 4, 0) if sy else rows(ryz[sy][sz], 3, 7)
            return packed + term(i, "11", lo, hi)

        came = shift(c, t00, t10, t01, t11)
        back = jnp.where(fluid, post[OPP_ALL[i]], pops[i])
        results.append(jnp.where(flag(i if i < 19 else i - 19), came, back))
    return results


KINDS = {
    "x": (2, 9, 8, 128),
    "y": (2, 5, 8, 128),
    "z": (2, 1, 8, 128),
    "xy": (2, 2, 1, 8, 128),
    "xz": (2, 2, 1, 8, 128),
    "yz": (2, 2, 1, 8, 128),
    "c": (2, 2, 2, 1, 128),
}


def kernel(counts, flow_hbm, phase_hbm, mask_hbm, flow_out, phase_out, *scratch):
    flow_in, phase_in, mask_in, flags, load_sem, send_sem, recv_sem = scratch[:7]
    names = list(KINDS)
    stage_refs = dict(zip(names, scratch[7:14]))
    recv_refs = dict(zip(names, scratch[14:21]))
    loads = [
        pltpu.make_async_copy(src, dst, load_sem.at[n])
        for n, (src, dst) in enumerate(
            ((phase_hbm, phase_in), (mask_hbm, mask_in), (flow_hbm, flow_in))
        )
    ]
    at = [lax.axis_index(a) for a in AXES]

    def exists(o):
        ok = None
        for dim, d in enumerate(o):
            if d:
                here = at[dim] > 0 if d < 0 else at[dim] < counts[dim] - 1
                ok = here if ok is None else jnp.logical_and(ok, here)
        return ok

    def peer(o):
        return tuple(at[dim] + d for dim, d in enumerate(o))

    barrier = pltpu.get_barrier_semaphore()
    for o in OFFS:

        @pl.when(exists(o))
        def _(o=o):
            pl.semaphore_signal(barrier, inc=1, device_id=peer(o), device_id_type=MESH)

    for load in loads:
        load.start()
    for o in OFFS:

        @pl.when(jnp.logical_not(exists(o)))
        def _(o=o):
            for step in range(STEPS):
                ref = part({k: r.at[step] for k, r in recv_refs.items()}, o, True)
                ref[...] = jnp.zeros(ref.shape, jnp.float32)

    near = 1
    for dim in range(3):
        near = near * (
            1
            + (at[dim] > 0).astype(jnp.int32)
            + (at[dim] < counts[dim] - 1).astype(jnp.int32)
        )

    def copy(step, o):
        stage = {k: r.at[step] for k, r in stage_refs.items() if k != "c"}
        recv = {k: r.at[step] for k, r in recv_refs.items()}
        first = step == 0
        if all(o):
            src = stage_refs["c"].at[step, (o[0] + 1) // 2, (o[1] + 1) // 2]
        else:
            src = part(stage, o, first)
        return pltpu.make_async_remote_copy(
            src_ref=src,
            dst_ref=part(recv, neg(o), first),
            send_sem=send_sem.at[step, SLOT[o]],
            recv_sem=recv_sem.at[step, SLOT[neg(o)]],
            device_id=peer(o),
            device_id_type=MESH,
        )

    def each(offs, action):
        for o in offs:

            @pl.when(exists(o))
            def _(o=o):
                action(o)

    faces = [o for o in OFFS if sum(map(abs, o)) == 1]
    rest = [o for o in OFFS if sum(map(abs, o)) > 1]
    for load in loads:
        load.wait()
    fluid = mask_in[...] == 1
    solid = jnp.where(fluid, 1.0, 0.0)
    pops = [flow_in[i] for i in range(19)] + [phase_in[j] for j in range(7)]
    for step in range(STEPS):
        stage = {k: r.at[step] for k, r in stage_refs.items()}
        recv = {k: r.at[step] for k, r in recv_refs.items()}
        local, _, masked = local_part(pops, fluid)
        flag_plane = solid if step == 0 else None

        def wait_recv(o, step=step, recv=recv):
            here = part(recv, o, step == 0)
            pltpu.make_async_remote_copy(
                src_ref=here,
                dst_ref=here,
                send_sem=send_sem.at[step, SLOT[o]],
                recv_sem=recv_sem.at[step, SLOT[o]],
                device_id=peer(o),
                device_id_type=MESH,
            ).wait_recv()

        def send(o, step=step):
            copy(step, o).start()

        fill_corners_and_edges(stage, local, masked, flag_plane)
        if step == 0:
            fill_faces(stage, local, masked, flag_plane)
            pl.semaphore_wait(barrier, near - 1)
            each(rest, send)
        else:
            each(rest, send)
            fill_faces(stage, local, masked, flag_plane)
        each(faces, send)
        if step == 1:
            each(OFFS, lambda o: copy(0, o).wait_send())

        def wait_faces(wait_recv=wait_recv):
            each(faces, wait_recv)

        def wait_rest(wait_recv=wait_recv, step=step, recv=recv):
            if step == 1:
                each(OFFS, lambda o: copy(1, o).wait_send())
            each(rest, wait_recv)
            if step == 0:
                for n, value in enumerate(source_flags(recv, solid)):
                    flags[n] = jnp.where(fluid, value, 0.0)
            return lambda i: flags[i - 1] > 0.5

        pops = finish_step(recv, pops, local, masked, fluid, wait_faces, wait_rest)
    for i in range(19):
        flow_out[i] = pops[i]
    for j in range(7):
        phase_out[j] = pops[19 + j]


def drain(flow_in, phase_in, flow_out, phase_out, sems):
    copies = [
        pltpu.make_async_copy(flow_in, flow_out, sems.at[0]),
        pltpu.make_async_copy(phase_in, phase_out, sems.at[1]),
    ]
    for copy in copies:
        copy.start()
    for copy in copies:
        copy.wait()


def solution(mesh):
    counts = [mesh.shape[a] for a in AXES]

    def shards(flow_pops, phase_pops, pore_mask):
        f32 = jnp.float32
        stage_kinds = dict(KINDS, c=(2, 2, 1, 128))
        shapes = (
            jax.ShapeDtypeStruct(flow_pops.shape, f32),
            jax.ShapeDtypeStruct(phase_pops.shape, f32),
        )
        vmem, hbm = pl.BlockSpec(memory_space=pltpu.VMEM), pl.BlockSpec(memory_space=pltpu.HBM)
        results = pl.pallas_call(
            lambda *refs: kernel(counts, *refs),
            out_shape=shapes,
            in_specs=[hbm] * 3,
            out_specs=(vmem, vmem),
            scratch_shapes=[
                pltpu.VMEM((19, 4, 8, 128), f32),
                pltpu.VMEM((7, 4, 8, 128), f32),
                pltpu.VMEM((4, 8, 128), jnp.int32),
                pltpu.VMEM((18, 4, 8, 128), f32),
                pltpu.SemaphoreType.DMA((3,)),
                pltpu.SemaphoreType.DMA((STEPS, 26)),
                pltpu.SemaphoreType.DMA((STEPS, 26)),
            ]
            + [pltpu.VMEM((STEPS, *shape), f32) for shape in stage_kinds.values()]
            + [pltpu.VMEM((STEPS, *shape), f32) for shape in KINDS.values()],
            compiler_params=pltpu.CompilerParams(
                collective_id=0, has_side_effects=True, vmem_limit_bytes=32 << 20
            ),
            name="lattice_steps",
        )(*(pltpu.with_memory_space_constraint(v, pltpu.HBM) for v in (flow_pops, phase_pops, pore_mask)))
        return pl.pallas_call(
            drain,
            out_shape=shapes,
            in_specs=[vmem, vmem],
            out_specs=(hbm, hbm),
            scratch_shapes=[pltpu.SemaphoreType.DMA((2,))],
            name="drain",
        )(*(pltpu.with_memory_space_constraint(v, pltpu.VMEM) for v in results))

    return jax.shard_map(
        shards,
        mesh=mesh,
        in_specs=(P(None, *AXES), P(None, *AXES), P(*AXES)),
        out_specs=(P(None, *AXES), P(None, *AXES)),
        check_vma=False,
    )
```

```python
import itertools

import jax
import jax.numpy as jnp
from jax import lax
from jax.experimental import pallas as pl
from jax.experimental.pallas import tpu as pltpu
from jax.sharding import PartitionSpec as P

STEPS = 2
MESH = pl.DeviceIdType.MESH
AXES = ("gx", "gy", "gz")
VEL = [
    (0, 0, 0),
    (1, 0, 0),
    (-1, 0, 0),
    (0, 1, 0),
    (0, -1, 0),
    (0, 0, 1),
    (0, 0, -1),
    (1, 1, 0),
    (-1, -1, 0),
    (1, -1, 0),
    (-1, 1, 0),
    (1, 0, 1),
    (-1, 0, -1),
    (1, 0, -1),
    (-1, 0, 1),
    (0, 1, 1),
    (0, -1, -1),
    (0, 1, -1),
    (0, -1, 1),
]
INDEX = {c: i for i, c in enumerate(VEL)}
OPP = [0, 2, 1, 4, 3, 6, 5, 8, 7, 10, 9, 12, 11, 14, 13, 16, 15, 18, 17]
VEL_ALL = VEL + VEL[:7]
OPP_ALL = OPP + [19 + j for j in OPP[:7]]
WT = [1.0 / 3.0] + [1.0 / 18.0] * 6 + [1.0 / 36.0] * 12
BT = [-2.0 / 9.0] + [1.0 / 54.0] * 6 + [1.0 / 27.0] * 12
OFFS = [o for o in itertools.product((-1, 0, 1), repeat=3) if any(o)]
FAR = sorted((o for o in OFFS if o[0] and o[2]), key=lambda o: o[1] != 0)
ALONG_Z = sorted((o for o in OFFS if o[2] and not o[0]), key=lambda o: o[1] != 0)
NEAR = sorted((o for o in OFFS if not o[2]), key=lambda o: (-sum(map(abs, o)), o[0] == 0))
OFFS = FAR + ALONG_Z + NEAR
SLOT = {o: n for n, o in enumerate(OFFS)}


def neg(o):
    return tuple(-d for d in o)


def crossing(dim, sign):
    flow = [i for i in range(19) if VEL[i][dim] == sign]
    return flow + [19 + INDEX[tuple(sign if d == dim else 0 for d in range(3))]]


def iota(dim):
    return lax.broadcasted_iota(jnp.int32, (1, 8, 128), dim)


def roll(v, shift, axis):
    size = v.shape[axis]
    shift %= size
    return pltpu.roll(v, shift, axis) if shift else v


def rows(v, frm, to):
    return roll(v, to - frm, 1)


def lanes(v, frm, to):
    return roll(v, to - frm, 2)


def sel(mask, a, b):
    return jnp.where(jnp.broadcast_to(mask, a.shape), a, b)


def local_part(pops, fluid):
    f, g = pops[:19], pops[19:]
    phase = ((g[0] + g[1]) + (g[2] + g[3])) + ((g[4] + g[5]) + g[6])
    masked = jnp.where(fluid, phase, 0.0)
    sums = {i: f[i] + f[OPP[i]] for i in range(1, 19, 2)}
    diff = {i: f[i] - f[OPP[i]] for i in range(1, 19, 2)}
    density = f[0]
    for i in range(1, 19, 2):
        density = density + sums[i]
    inv = 1.0 / density
    mom = []
    for dim in range(3):
        total = None
        for i in range(1, 19, 2):
            s = VEL[i][dim]
            if s:
                term = diff[i]
                total = term if total is None else (total + term if s > 0 else total - term)
        mom.append(total)
    flow = [m * inv for m in mom]
    speed_sq = flow[0] * flow[0] + flow[1] * flow[1] + flow[2] * flow[2]
    omega = 1.0 / (0.8 + 0.2 * phase)
    keep = 1.0 - omega
    base = omega * density
    even0 = base * (1.0 - 1.5 * speed_sq)
    out = [None] * 26
    out[0] = keep * f[0] + WT[0] * even0
    for i in range(1, 19, 2):
        c = VEL[i]
        along = None
        for dim in range(3):
            if c[dim]:
                term = flow[dim]
                along = term if along is None else (along + term if c[dim] > 0 else along - term)
        even = WT[i] * even0 + (4.5 * WT[i]) * base * (along * along)
        odd = (3.0 * WT[i]) * base * along
        out[i] = keep * f[i] + (even + odd)
        out[i + 1] = keep * f[i + 1] + (even - odd)
    out[19] = (1.25 * 0.25) * phase - 0.25 * g[0]
    eighth = (1.25 * 0.125) * phase
    for dim in range(3):
        odd = 4.0 * eighth * flow[dim]
        out[20 + 2 * dim] = (eighth + odd) - 0.25 * g[1 + 2 * dim]
        out[21 + 2 * dim] = (eighth - odd) - 0.25 * g[2 + 2 * dim]
    return out, phase, masked


def merge_planes(v, block, offset):
    lane = iota(2)
    acc = roll(v[0:1], offset, 2)
    for x in range(1, 4):
        acc = sel(lane >= block * x, roll(v[x : x + 1], block * x + offset, 2), acc)
    return acc


def split_planes(v, block, offset):
    return join(*(roll(v, -(block * x + offset), 2) for x in range(4)))


def edge_sides():
    for sa, sb in itertools.product((0, 1), repeat=2):
        near, far = (3, 2) if sa else (0, 1)
        yield sa, sb, slice(near, near + 1), slice(far, far + 1), 2 * sa - 1, 2 * sb - 1


def fill_far(stage, local, masked, solid):
    lane = iota(2)
    for sa, sb, xs, fs, ga, gb in edge_sides():
        acc = masked[xs]
        edge, pop, flag, deep = (127, 63, 62, 61) if sb else (0, 64, 65, 66)
        acc = sel(lane == pop, lanes(local[INDEX[(ga, 0, gb)]][xs], edge, pop), acc)
        acc = sel(lane == deep, lanes(masked[fs], edge, deep), acc)
        if solid is not None:
            acc = sel(lane == flag, lanes(solid[xs], edge, flag), acc)
        stage["xz"][sa, sb] = acc
        edge = 7 if sb else 0
        stage["c"][sa, sb] = masked[xs][0][edge : edge + 1]


def fill_along_z(stage, local, masked, solid):
    row, lane = iota(1), iota(2)
    for side, sign in ((0, -1), (1, 1)):
        acc = masked
        edge, first = (127, 0) if side else (0, 2)
        for k, i in enumerate(crossing(2, sign)):
            acc = sel(lane == first + k, lanes(local[i], edge, first + k), acc)
        if solid is not None:
            acc = sel(lane == first + 6, lanes(solid, edge, first + 6), acc)
        stage["z"][side] = merge_planes(acc, 16, 2 * side)
    for sa, sb, _, _, ga, gb in edge_sides():
        acc = masked
        edge, pop, flag = (7, 3, 2) if sa else (0, 4, 5)
        acc = sel(row == pop, rows(local[INDEX[(0, ga, gb)]], edge, pop), acc)
        if solid is not None:
            acc = sel(row == flag, rows(solid, edge, flag), acc)
        stage["yz"][sa, sb] = merge_planes(acc, 2, 2 * sb)


def fill_near(stage, local, masked, solid):
    row = iota(1)
    for sa, sb, xs, fs, ga, gb in edge_sides():
        acc = masked[xs]
        edge, pop, flag, deep = (7, 3, 2, 4) if sb else (0, 4, 5, 3)
        acc = sel(row == pop, rows(local[INDEX[(ga, gb, 0)]][xs], edge, pop), acc)
        acc = sel(row == deep, rows(masked[fs], edge, deep), acc)
        if solid is not None:
            acc = sel(row == flag, rows(solid[xs], edge, flag), acc)
        stage["xy"][sa, sb] = acc
    for side, sign in ((0, -1), (1, 1)):
        near, far = (3, 2) if side else (0, 1)
        out = stage["x"]
        for k, i in enumerate(crossing(0, sign)):
            out[side, k] = local[i][near]
        out[side, 6] = masked[near]
        out[side, 7] = masked[far]
        if solid is not None:
            out[side, 8] = solid[near]
        acc = masked
        edge, first = (7, 0) if side else (0, 2)
        for k, i in enumerate(crossing(1, sign)):
            acc = sel(row == first + k, rows(local[i], edge, first + k), acc)
        stage["y"][side, 0:4] = acc
        if solid is not None:
            acc = rows(solid[0:1], edge, 0)
            for x in range(1, 4):
                acc = sel(row == x, rows(solid[x : x + 1], edge, x), acc)
            stage["y"][side, 4:5] = acc


def part(bufs, o, first):
    a, b, c = ((d + 1) // 2 for d in o)
    kind = tuple(d != 0 for d in o)
    if kind == (True, False, False):
        return bufs["x"].at[a, pl.ds(0, 9 if first else 8)]
    if kind == (False, True, False):
        return bufs["y"].at[b, pl.ds(0, 5 if first else 4)]
    if kind == (False, False, True):
        return bufs["z"].at[c]
    if kind == (True, True, False):
        return bufs["xy"].at[a, b]
    if kind == (True, False, True):
        return bufs["xz"].at[a, c]
    if kind == (False, True, True):
        return bufs["yz"].at[b, c]
    return bufs["c"].at[a, b, c]


def pair_shift(own, halo, sign, axis):
    size = own.shape[axis]
    at = iota(axis)
    if sign > 0:
        return sel(at == 0, roll(halo, 1, axis), roll(own, 1, axis))
    return sel(at == size - 1, roll(halo, -1, axis), roll(own, -1, axis))


def shift(c, t00, t10, t01, t11):
    if c[1]:
        t00 = pair_shift(t00(), t10(), c[1], 1)
        halo = (lambda: pair_shift(t01(), t11(), c[1], 1)) if c[2] else None
    else:
        t00, halo = t00(), t01
    return pair_shift(t00, halo(), c[2], 2) if c[2] else t00


def join(*parts):
    return jnp.concatenate(parts, axis=0)


def minus_plus(minus, plus, axis):
    at = iota(axis)
    half = 4 if axis == 1 else 64
    return sel(at < half, plus, minus)


def along_x(c, own, low, high):
    if c[0] > 0:
        return join(low(), own[0:3])
    if c[0] < 0:
        return join(own[1:4], high())
    return own


def source_flags(recv, solid):
    y = [recv["y"][s, 4:5] for s in (0, 1)]
    y = join(*(minus_plus(rows(y[0], x, 7), rows(y[1], x, 0), 1) for x in range(4)))
    z = [split_planes(recv["z"][s], 16, 2 * (1 - s)) for s in (0, 1)]
    z = minus_plus(lanes(z[0], 6, 127), lanes(z[1], 8, 0), 2)
    x = [recv["x"][s, 8:9] for s in (0, 1)]
    xy = [
        minus_plus(rows(recv["xy"][s, 0], 2, 7), rows(recv["xy"][s, 1], 5, 0), 1) for s in (0, 1)
    ]
    xz = [
        minus_plus(lanes(recv["xz"][s, 0], 62, 127), lanes(recv["xz"][s, 1], 65, 0), 2)
        for s in (0, 1)
    ]
    yz = [
        minus_plus(rows(recv["yz"][0, s], 2, 7), rows(recv["yz"][1, s], 5, 0), 1) for s in (0, 1)
    ]
    yz = [split_planes(yz[s], 2, 2 * (1 - s)) for s in (0, 1)]
    yz = minus_plus(yz[0], yz[1], 2)
    flags = []
    for i in range(1, 19):
        c = VEL[i]
        flags.append(
            shift(
                c,
                lambda: along_x(c, solid, lambda: x[0], lambda: x[1]),
                lambda: along_x(c, y, lambda: xy[0], lambda: xy[1]),
                lambda: along_x(c, z, lambda: xz[0], lambda: xz[1]),
                lambda: yz,
            )
        )
    return flags


def finish_step(recv, pops, local, masked, fluid, wait_faces, wait_rest):
    def grads(own, in_y, in_z):
        mid = own[1:-1]
        gx = 0.5 * (own[2:] - own[:-2])
        gy = 0.5 * (pair_shift(mid, in_y, -1, 1) - pair_shift(mid, in_y, 1, 1))
        gz = 0.5 * (pair_shift(mid, in_z, -1, 2) - pair_shift(mid, in_z, 1, 2))
        square = gx * gx + gy * gy + gz * gz + 0.01
        inv = lax.rsqrt(square)
        return ((gx, gy, gz), inv, square * inv, mid)

    tiles, known = {}, {}
    first_plane = {"00": 0, "low": -1, "high": 4, "10": -1, "01": -1, "11": 0}

    def cut(v, name, lo, hi):
        base = first_plane[name]
        return v[lo - base : hi - base + 1]

    def term(i, name, lo, hi):
        grad, inv, mag, phase = tiles[name]
        if i >= 19:
            dim, sign = (i - 20) // 2, 1 - 2 * ((i - 20) % 2)
            key = ("g", dim, name, lo, hi)
            if key not in known:
                p, d, r = (cut(v, name, lo, hi) for v in (phase, grad[dim], inv))
                known[key] = (0.875 * 0.125) * ((1.0 - p * p) * (d * r))
            return known[key] if sign > 0 else -known[key]
        pair = i if i % 2 else i - 1
        key = (pair, name, lo, hi)
        if key not in known:
            cross = None
            for dim in range(3):
                if VEL[pair][dim]:
                    d = cut(grad[dim], name, lo, hi)
                    cross = (
                        d if cross is None else (cross + d if VEL[pair][dim] > 0 else cross - d)
                    )
            r, m = cut(inv, name, lo, hi), cut(mag, name, lo, hi)
            known[key] = (0.5 * WT[pair]) * (cross * cross * r) - (0.5 * BT[pair]) * m
        return known[key]

    wait_faces()
    rx, ry = recv["x"], recv["y"]
    rz = [split_planes(recv["z"][s], 16, 2 * (1 - s)) for s in (0, 1)]
    y_faces = [ry[s, 0:4] for s in (0, 1)]
    m00 = join(rx[0, 7:8], rx[0, 6:7], masked, rx[1, 6:7], rx[1, 7:8])
    m10 = minus_plus(y_faces[0], y_faces[1], 1)
    m01 = minus_plus(rz[0], rz[1], 2)
    tiles["00"] = grads(m00[1:-1], m10, m01)
    post = [None] * 26
    post[0] = local[0] - (0.5 * BT[0]) * tiles["00"][2]
    post[19] = local[19]
    for i in itertools.chain(range(1, 19), range(20, 26)):
        post[i] = local[i] + term(i, "00", 0, 3)

    flag = wait_rest()
    rxy, rxz, rc = recv["xy"], recv["xz"], recv["c"]
    ryz = [[split_planes(recv["yz"][b, c], 2, 2 * (1 - c)) for c in (0, 1)] for b in (0, 1)]

    def deep_xy(s):
        return minus_plus(rows(rxy[s, 0], 4, 7), rows(rxy[s, 1], 3, 0), 1)

    def deep_xz(s):
        return minus_plus(lanes(rxz[s, 0], 61, 127), lanes(rxz[s, 1], 66, 0), 2)

    def near_xy(s):
        return minus_plus(rxy[s, 0], rxy[s, 1], 1)

    def near_xz(s):
        return minus_plus(rxz[s, 0], rxz[s, 1], 2)

    def corner(s):
        line = [[jnp.broadcast_to(rc[s, b, c][None], (1, 8, 128)) for c in (0, 1)] for b in (0, 1)]
        return minus_plus(minus_plus(*line[0], 2), minus_plus(*line[1], 2), 1)

    m10 = join(deep_xy(0), near_xy(0), m10, near_xy(1), deep_xy(1))
    m01 = join(deep_xz(0), near_xz(0), m01, near_xz(1), deep_xz(1))
    m11 = join(
        corner(0), minus_plus(minus_plus(*ryz[0], 2), minus_plus(*ryz[1], 2), 1), corner(1)
    )
    tiles["low"] = grads(m00[0:3], m10[1:2], m01[1:2])
    tiles["high"] = grads(m00[5:8], m10[6:7], m01[6:7])
    tiles["10"] = grads(m10, m00[1:-1], m11)
    tiles["01"] = grads(m01, m11, m00[1:-1])
    tiles["11"] = grads(m11, m01[2:-2], m10[2:-2])

    results = []
    for i in range(26):
        if i in (0, 19):
            results.append(jnp.where(fluid, post[i], pops[i]))
            continue
        c = VEL_ALL[i]
        lo, hi = -c[0], 3 - c[0]
        sx, sy, sz = ((1 - d) // 2 for d in c)

        def from_x():
            k, plane = crossing(0, c[0]).index(i), 5 * sx - 1
            return rx[sx, k : k + 1] + term(i, "high" if sx else "low", plane, plane)

        def t00():
            return along_x(c, post[i], from_x, from_x)

        def t10():
            k = crossing(1, c[1]).index(i)
            packed = rows(y_faces[sy], k + 2, 0) if sy else rows(y_faces[sy], k, 7)

            def edge():
                return rows(rxy[sx, sy], 4, 0) if sy else rows(rxy[sx, sy], 3, 7)

            return along_x(c, packed, edge, edge) + term(i, "10", lo, hi)

        def t01():
            k = crossing(2, c[2]).index(i)
            packed = lanes(rz[sz], k + 2, 0) if sz else lanes(rz[sz], k, 127)

            def edge():
                return lanes(rxz[sx, sz], 64, 0) if sz else lanes(rxz[sx, sz], 63, 127)

            return along_x(c, packed, edge, edge) + term(i, "01", lo, hi)

        def t11():
            packed = rows(ryz[sy][sz], 4, 0) if sy else rows(ryz[sy][sz], 3, 7)
            return packed + term(i, "11", lo, hi)

        came = shift(c, t00, t10, t01, t11)
        back = jnp.where(fluid, post[OPP_ALL[i]], pops[i])
        results.append(jnp.where(flag(i if i < 19 else i - 19), came, back))
    return results


KINDS = {
    "x": (2, 9, 8, 128),
    "y": (2, 5, 8, 128),
    "z": (2, 1, 8, 128),
    "xy": (2, 2, 1, 8, 128),
    "xz": (2, 2, 1, 8, 128),
    "yz": (2, 2, 1, 8, 128),
    "c": (2, 2, 2, 1, 128),
}


def kernel(counts, flow_hbm, phase_hbm, mask_hbm, flow_out, phase_out, *scratch):
    flow_in, phase_in, mask_in, flags, load_sem, send_sem, recv_sem = scratch[:7]
    names = list(KINDS)
    stage_refs = dict(zip(names, scratch[7:14]))
    recv_refs = dict(zip(names, scratch[14:21]))
    loads = [
        pltpu.make_async_copy(src, dst, load_sem.at[n])
        for n, (src, dst) in enumerate(
            ((phase_hbm, phase_in), (mask_hbm, mask_in), (flow_hbm, flow_in))
        )
    ]
    at = [lax.axis_index(a) for a in AXES]

    def exists(o):
        ok = None
        for dim, d in enumerate(o):
            if d:
                here = at[dim] > 0 if d < 0 else at[dim] < counts[dim] - 1
                ok = here if ok is None else jnp.logical_and(ok, here)
        return ok

    def peer(o):
        return tuple(at[dim] + d for dim, d in enumerate(o))

    barrier = pltpu.get_barrier_semaphore()
    for o in OFFS:

        @pl.when(exists(o))
        def _(o=o):
            pl.semaphore_signal(barrier, inc=1, device_id=peer(o), device_id_type=MESH)

    for load in loads:
        load.start()
    for o in OFFS:

        @pl.when(jnp.logical_not(exists(o)))
        def _(o=o):
            for step in range(STEPS):
                ref = part({k: r.at[step] for k, r in recv_refs.items()}, o, True)
                ref[...] = jnp.zeros(ref.shape, jnp.float32)

    near = 1
    for dim in range(3):
        near = near * (
            1
            + (at[dim] > 0).astype(jnp.int32)
            + (at[dim] < counts[dim] - 1).astype(jnp.int32)
        )

    def copy(step, o):
        stage = {k: r.at[step] for k, r in stage_refs.items() if k != "c"}
        recv = {k: r.at[step] for k, r in recv_refs.items()}
        first = step == 0
        if all(o):
            src = stage_refs["c"].at[step, (o[0] + 1) // 2, (o[1] + 1) // 2]
        else:
            src = part(stage, o, first)
        return pltpu.make_async_remote_copy(
            src_ref=src,
            dst_ref=part(recv, neg(o), first),
            send_sem=send_sem.at[step, SLOT[o]],
            recv_sem=recv_sem.at[step, SLOT[neg(o)]],
            device_id=peer(o),
            device_id_type=MESH,
        )

    def each(offs, action):
        for o in offs:

            @pl.when(exists(o))
            def _(o=o):
                action(o)

    faces = [o for o in reversed(OFFS) if sum(map(abs, o)) == 1]
    rest = [o for o in reversed(OFFS) if sum(map(abs, o)) > 1]
    for load in loads:
        load.wait()
    fluid = mask_in[...] == 1
    solid = jnp.where(fluid, 1.0, 0.0)
    pops = [flow_in[i] for i in range(19)] + [phase_in[j] for j in range(7)]
    for step in range(STEPS):
        stage = {k: r.at[step] for k, r in stage_refs.items()}
        recv = {k: r.at[step] for k, r in recv_refs.items()}
        local, _, masked = local_part(pops, fluid)
        flag_plane = solid if step == 0 else None

        def wait_recv(o, step=step, recv=recv):
            here = part(recv, o, step == 0)
            pltpu.make_async_remote_copy(
                src_ref=here,
                dst_ref=here,
                send_sem=send_sem.at[step, SLOT[o]],
                recv_sem=recv_sem.at[step, SLOT[o]],
                device_id=peer(o),
                device_id_type=MESH,
            ).wait_recv()

        def send(o, step=step):
            copy(step, o).start()

        groups = ((fill_far, FAR), (fill_along_z, ALONG_Z), (fill_near, NEAR))
        if step == 0:
            for fill, _ in groups:
                fill(stage, local, masked, flag_plane)
            pl.semaphore_wait(barrier, near - 1)
        for fill, offs in groups:
            if step > 0:
                fill(stage, local, masked, flag_plane)
            each(offs, send)
        if step == 1:
            each(OFFS, lambda o: copy(0, o).wait_send())

        def wait_faces(wait_recv=wait_recv):
            each(faces, wait_recv)

        def wait_rest(wait_recv=wait_recv, step=step, recv=recv):
            if step == 1:
                each(OFFS, lambda o: copy(1, o).wait_send())
            each(rest, wait_recv)
            if step == 0:
                for n, value in enumerate(source_flags(recv, solid)):
                    flags[n] = jnp.where(fluid, value, 0.0)
            return lambda i: flags[i - 1] > 0.5

        pops = finish_step(recv, pops, local, masked, fluid, wait_faces, wait_rest)
    for i in range(19):
        flow_out[i] = pops[i]
    for j in range(7):
        phase_out[j] = pops[19 + j]


def drain(flow_in, phase_in, flow_out, phase_out, sems):
    copies = [
        pltpu.make_async_copy(flow_in, flow_out, sems.at[0]),
        pltpu.make_async_copy(phase_in, phase_out, sems.at[1]),
    ]
    for copy in copies:
        copy.start()
    for copy in copies:
        copy.wait()


def solution(mesh):
    counts = [mesh.shape[a] for a in AXES]

    def shards(flow_pops, phase_pops, pore_mask):
        f32 = jnp.float32
        stage_kinds = dict(KINDS, c=(2, 2, 1, 128))
        shapes = (
            jax.ShapeDtypeStruct(flow_pops.shape, f32),
            jax.ShapeDtypeStruct(phase_pops.shape, f32),
        )
        vmem, hbm = pl.BlockSpec(memory_space=pltpu.VMEM), pl.BlockSpec(memory_space=pltpu.HBM)
        results = pl.pallas_call(
            lambda *refs: kernel(counts, *refs),
            out_shape=shapes,
            in_specs=[hbm] * 3,
            out_specs=(vmem, vmem),
            scratch_shapes=[
                pltpu.VMEM((19, 4, 8, 128), f32),
                pltpu.VMEM((7, 4, 8, 128), f32),
                pltpu.VMEM((4, 8, 128), jnp.int32),
                pltpu.VMEM((18, 4, 8, 128), f32),
                pltpu.SemaphoreType.DMA((3,)),
                pltpu.SemaphoreType.DMA((STEPS, 26)),
                pltpu.SemaphoreType.DMA((STEPS, 26)),
            ]
            + [pltpu.VMEM((STEPS, *shape), f32) for shape in stage_kinds.values()]
            + [pltpu.VMEM((STEPS, *shape), f32) for shape in KINDS.values()],
            compiler_params=pltpu.CompilerParams(
                collective_id=0, has_side_effects=True, vmem_limit_bytes=32 << 20
            ),
            name="lattice_steps",
        )(*(pltpu.with_memory_space_constraint(v, pltpu.HBM) for v in (flow_pops, phase_pops, pore_mask)))
        return pl.pallas_call(
            drain,
            out_shape=shapes,
            in_specs=[vmem, vmem],
            out_specs=(hbm, hbm),
            scratch_shapes=[pltpu.SemaphoreType.DMA((2,))],
            name="drain",
        )(*(pltpu.with_memory_space_constraint(v, pltpu.VMEM) for v in results))

    return jax.shard_map(
        shards,
        mesh=mesh,
        in_specs=(P(None, *AXES), P(None, *AXES), P(*AXES)),
        out_specs=(P(None, *AXES), P(None, *AXES)),
        check_vma=False,
    )
```

```python
import itertools

import jax
import jax.numpy as jnp
from jax import lax
from jax.experimental import pallas as pl
from jax.experimental.pallas import tpu as pltpu
from jax.sharding import PartitionSpec as P

STEPS = 2
MESH = pl.DeviceIdType.MESH
AXES = ("gx", "gy", "gz")
VEL = [
    (0, 0, 0),
    (1, 0, 0),
    (-1, 0, 0),
    (0, 1, 0),
    (0, -1, 0),
    (0, 0, 1),
    (0, 0, -1),
    (1, 1, 0),
    (-1, -1, 0),
    (1, -1, 0),
    (-1, 1, 0),
    (1, 0, 1),
    (-1, 0, -1),
    (1, 0, -1),
    (-1, 0, 1),
    (0, 1, 1),
    (0, -1, -1),
    (0, 1, -1),
    (0, -1, 1),
]
INDEX = {c: i for i, c in enumerate(VEL)}
OPP = [0, 2, 1, 4, 3, 6, 5, 8, 7, 10, 9, 12, 11, 14, 13, 16, 15, 18, 17]
VEL_ALL = VEL + VEL[:7]
OPP_ALL = OPP + [19 + j for j in OPP[:7]]
WT = [1.0 / 3.0] + [1.0 / 18.0] * 6 + [1.0 / 36.0] * 12
BT = [-2.0 / 9.0] + [1.0 / 54.0] * 6 + [1.0 / 27.0] * 12
OFFS = [o for o in itertools.product((-1, 0, 1), repeat=3) if any(o)]
FAR = sorted((o for o in OFFS if o[0] and o[2]), key=lambda o: o[1] != 0)
ALONG_Z = sorted((o for o in OFFS if o[2] and not o[0]), key=lambda o: o[1] != 0)
NEAR = sorted((o for o in OFFS if not o[2]), key=lambda o: (-sum(map(abs, o)), o[0] == 0))
OFFS = FAR + ALONG_Z + NEAR
SLOT = {o: n for n, o in enumerate(OFFS)}


def neg(o):
    return tuple(-d for d in o)


def crossing(dim, sign):
    flow = [i for i in range(19) if VEL[i][dim] == sign]
    return flow + [19 + INDEX[tuple(sign if d == dim else 0 for d in range(3))]]


def iota(dim):
    return lax.broadcasted_iota(jnp.int32, (1, 8, 128), dim)


def roll(v, shift, axis):
    size = v.shape[axis]
    shift %= size
    return pltpu.roll(v, shift, axis) if shift else v


def rows(v, frm, to):
    return roll(v, to - frm, 1)


def lanes(v, frm, to):
    return roll(v, to - frm, 2)


def sel(mask, a, b):
    return jnp.where(jnp.broadcast_to(mask, a.shape), a, b)


def local_part(pops, fluid):
    f, g = pops[:19], pops[19:]
    phase = ((g[0] + g[1]) + (g[2] + g[3])) + ((g[4] + g[5]) + g[6])
    masked = jnp.where(fluid, phase, 0.0)
    sums = {i: f[i] + f[OPP[i]] for i in range(1, 19, 2)}
    diff = {i: f[i] - f[OPP[i]] for i in range(1, 19, 2)}
    density = f[0]
    for i in range(1, 19, 2):
        density = density + sums[i]
    inv = 1.0 / density
    mom = []
    for dim in range(3):
        total = None
        for i in range(1, 19, 2):
            s = VEL[i][dim]
            if s:
                term = diff[i]
                total = term if total is None else (total + term if s > 0 else total - term)
        mom.append(total)
    flow = [m * inv for m in mom]
    speed_sq = flow[0] * flow[0] + flow[1] * flow[1] + flow[2] * flow[2]
    omega = 1.0 / (0.8 + 0.2 * phase)
    keep = 1.0 - omega
    base = omega * density
    even0 = base * (1.0 - 1.5 * speed_sq)
    out = [None] * 26
    out[0] = keep * f[0] + WT[0] * even0
    for i in range(1, 19, 2):
        c = VEL[i]
        along = None
        for dim in range(3):
            if c[dim]:
                term = flow[dim]
                along = term if along is None else (along + term if c[dim] > 0 else along - term)
        even = WT[i] * even0 + (4.5 * WT[i]) * base * (along * along)
        odd = (3.0 * WT[i]) * base * along
        out[i] = keep * f[i] + (even + odd)
        out[i + 1] = keep * f[i + 1] + (even - odd)
    out[19] = (1.25 * 0.25) * phase - 0.25 * g[0]
    eighth = (1.25 * 0.125) * phase
    for dim in range(3):
        odd = 4.0 * eighth * flow[dim]
        out[20 + 2 * dim] = (eighth + odd) - 0.25 * g[1 + 2 * dim]
        out[21 + 2 * dim] = (eighth - odd) - 0.25 * g[2 + 2 * dim]
    return out, phase, masked


def merge_planes(v, block, offset):
    lane = iota(2)
    acc = roll(v[0:1], offset, 2)
    for x in range(1, 4):
        acc = sel(lane >= block * x, roll(v[x : x + 1], block * x + offset, 2), acc)
    return acc


def split_planes(v, block, offset):
    return join(*(roll(v, -(block * x + offset), 2) for x in range(4)))


def edge_sides():
    for sa, sb in itertools.product((0, 1), repeat=2):
        near, far = (3, 2) if sa else (0, 1)
        yield sa, sb, slice(near, near + 1), slice(far, far + 1), 2 * sa - 1, 2 * sb - 1


def fill_far(stage, local, masked, solid):
    lane = iota(2)
    for sa, sb, xs, fs, ga, gb in edge_sides():
        acc = masked[xs]
        edge, pop, flag, deep = (127, 63, 62, 61) if sb else (0, 64, 65, 66)
        acc = sel(lane == pop, lanes(local[INDEX[(ga, 0, gb)]][xs], edge, pop), acc)
        acc = sel(lane == deep, lanes(masked[fs], edge, deep), acc)
        if solid is not None:
            acc = sel(lane == flag, lanes(solid[xs], edge, flag), acc)
        stage["xz"][sa, sb] = acc
        edge = 7 if sb else 0
        stage["c"][sa, sb] = masked[xs][0][edge : edge + 1]


def fill_along_z(stage, local, masked, solid):
    row, lane = iota(1), iota(2)
    for side, sign in ((0, -1), (1, 1)):
        acc = masked
        edge, first = (127, 0) if side else (0, 2)
        for k, i in enumerate(crossing(2, sign)):
            acc = sel(lane == first + k, lanes(local[i], edge, first + k), acc)
        if solid is not None:
            acc = sel(lane == first + 6, lanes(solid, edge, first + 6), acc)
        stage["z"][side] = merge_planes(acc, 16, 2 * side)
    for sa, sb, _, _, ga, gb in edge_sides():
        acc = masked
        edge, pop, flag = (7, 3, 2) if sa else (0, 4, 5)
        acc = sel(row == pop, rows(local[INDEX[(0, ga, gb)]], edge, pop), acc)
        if solid is not None:
            acc = sel(row == flag, rows(solid, edge, flag), acc)
        stage["yz"][sa, sb] = merge_planes(acc, 2, 2 * sb)


def fill_near(stage, local, masked, solid):
    row = iota(1)
    for sa, sb, xs, fs, ga, gb in edge_sides():
        acc = masked[xs]
        edge, pop, flag, deep = (7, 3, 2, 4) if sb else (0, 4, 5, 3)
        acc = sel(row == pop, rows(local[INDEX[(ga, gb, 0)]][xs], edge, pop), acc)
        acc = sel(row == deep, rows(masked[fs], edge, deep), acc)
        if solid is not None:
            acc = sel(row == flag, rows(solid[xs], edge, flag), acc)
        stage["xy"][sa, sb] = acc
    for side, sign in ((0, -1), (1, 1)):
        near, far = (3, 2) if side else (0, 1)
        out = stage["x"]
        for k, i in enumerate(crossing(0, sign)):
            out[side, k] = local[i][near]
        out[side, 6] = masked[near]
        out[side, 7] = masked[far]
        if solid is not None:
            out[side, 8] = solid[near]
        acc = masked
        edge, first = (7, 0) if side else (0, 2)
        for k, i in enumerate(crossing(1, sign)):
            acc = sel(row == first + k, rows(local[i], edge, first + k), acc)
        stage["y"][side, 0:4] = acc
        if solid is not None:
            acc = rows(solid[0:1], edge, 0)
            for x in range(1, 4):
                acc = sel(row == x, rows(solid[x : x + 1], edge, x), acc)
            stage["y"][side, 4:5] = acc


def part(bufs, o, first):
    a, b, c = ((d + 1) // 2 for d in o)
    kind = tuple(d != 0 for d in o)
    if kind == (True, False, False):
        return bufs["x"].at[a, pl.ds(0, 9 if first else 8)]
    if kind == (False, True, False):
        return bufs["y"].at[b, pl.ds(0, 5 if first else 4)]
    if kind == (False, False, True):
        return bufs["z"].at[c]
    if kind == (True, True, False):
        return bufs["xy"].at[a, b]
    if kind == (True, False, True):
        return bufs["xz"].at[a, c]
    if kind == (False, True, True):
        return bufs["yz"].at[b, c]
    return bufs["c"].at[a, b, c]


def pair_shift(own, halo, sign, axis):
    size = own.shape[axis]
    at = iota(axis)
    if sign > 0:
        return sel(at == 0, roll(halo, 1, axis), roll(own, 1, axis))
    return sel(at == size - 1, roll(halo, -1, axis), roll(own, -1, axis))


def shift(c, t00, t10, t01, t11):
    if c[1]:
        t00 = pair_shift(t00(), t10(), c[1], 1)
        halo = (lambda: pair_shift(t01(), t11(), c[1], 1)) if c[2] else None
    else:
        t00, halo = t00(), t01
    return pair_shift(t00, halo(), c[2], 2) if c[2] else t00


def join(*parts):
    return jnp.concatenate(parts, axis=0)


def minus_plus(minus, plus, axis):
    at = iota(axis)
    half = 4 if axis == 1 else 64
    return sel(at < half, plus, minus)


def along_x(c, own, low, high):
    if c[0] > 0:
        return join(low(), own[0:3])
    if c[0] < 0:
        return join(own[1:4], high())
    return own


def source_flags(recv, solid):
    y = [recv["y"][s, 4:5] for s in (0, 1)]
    y = join(*(minus_plus(rows(y[0], x, 7), rows(y[1], x, 0), 1) for x in range(4)))
    z = [split_planes(recv["z"][s], 16, 2 * (1 - s)) for s in (0, 1)]
    z = minus_plus(lanes(z[0], 6, 127), lanes(z[1], 8, 0), 2)
    x = [recv["x"][s, 8:9] for s in (0, 1)]
    xy = [
        minus_plus(rows(recv["xy"][s, 0], 2, 7), rows(recv["xy"][s, 1], 5, 0), 1) for s in (0, 1)
    ]
    xz = [
        minus_plus(lanes(recv["xz"][s, 0], 62, 127), lanes(recv["xz"][s, 1], 65, 0), 2)
        for s in (0, 1)
    ]
    yz = [
        minus_plus(rows(recv["yz"][0, s], 2, 7), rows(recv["yz"][1, s], 5, 0), 1) for s in (0, 1)
    ]
    yz = [split_planes(yz[s], 2, 2 * (1 - s)) for s in (0, 1)]
    yz = minus_plus(yz[0], yz[1], 2)
    flags = []
    for i in range(1, 19):
        c = VEL[i]
        flags.append(
            shift(
                c,
                lambda: along_x(c, solid, lambda: x[0], lambda: x[1]),
                lambda: along_x(c, y, lambda: xy[0], lambda: xy[1]),
                lambda: along_x(c, z, lambda: xz[0], lambda: xz[1]),
                lambda: yz,
            )
        )
    return flags


def finish_step(recv, pops, local, masked, fluid, wait_faces, wait_rest):
    def grads(own, in_y, in_z):
        mid = own[1:-1]
        gx = 0.5 * (own[2:] - own[:-2])
        gy = 0.5 * (pair_shift(mid, in_y, -1, 1) - pair_shift(mid, in_y, 1, 1))
        gz = 0.5 * (pair_shift(mid, in_z, -1, 2) - pair_shift(mid, in_z, 1, 2))
        square = gx * gx + gy * gy + gz * gz + 0.01
        inv = lax.rsqrt(square)
        return ((gx, gy, gz), inv, square * inv, mid)

    tiles, known = {}, {}
    first_plane = {"00": 0, "low": -1, "high": 4, "10": -1, "01": -1, "11": 0}

    def cut(v, name, lo, hi):
        base = first_plane[name]
        return v[lo - base : hi - base + 1]

    def term(i, name, lo, hi):
        grad, inv, mag, phase = tiles[name]
        if i >= 19:
            dim, sign = (i - 20) // 2, 1 - 2 * ((i - 20) % 2)
            key = ("g", dim, name, lo, hi)
            if key not in known:
                p, d, r = (cut(v, name, lo, hi) for v in (phase, grad[dim], inv))
                known[key] = (0.875 * 0.125) * ((1.0 - p * p) * (d * r))
            return known[key] if sign > 0 else -known[key]
        pair = i if i % 2 else i - 1
        key = (pair, name, lo, hi)
        if key not in known:
            cross = None
            for dim in range(3):
                if VEL[pair][dim]:
                    d = cut(grad[dim], name, lo, hi)
                    cross = (
                        d if cross is None else (cross + d if VEL[pair][dim] > 0 else cross - d)
                    )
            r, m = cut(inv, name, lo, hi), cut(mag, name, lo, hi)
            known[key] = (0.5 * WT[pair]) * (cross * cross * r) - (0.5 * BT[pair]) * m
        return known[key]

    wait_faces()
    rx, ry = recv["x"], recv["y"]
    rz = [split_planes(recv["z"][s], 16, 2 * (1 - s)) for s in (0, 1)]
    y_faces = [ry[s, 0:4] for s in (0, 1)]
    m00 = join(rx[0, 7:8], rx[0, 6:7], masked, rx[1, 6:7], rx[1, 7:8])
    m10 = minus_plus(y_faces[0], y_faces[1], 1)
    m01 = minus_plus(rz[0], rz[1], 2)
    tiles["00"] = grads(m00[1:-1], m10, m01)
    post = [None] * 26
    post[0] = local[0] - (0.5 * BT[0]) * tiles["00"][2]
    post[19] = local[19]
    for i in itertools.chain(range(1, 19), range(20, 26)):
        post[i] = local[i] + term(i, "00", 0, 3)

    flag = wait_rest()
    rxy, rxz, rc = recv["xy"], recv["xz"], recv["c"]
    ryz = [[split_planes(recv["yz"][b, c], 2, 2 * (1 - c)) for c in (0, 1)] for b in (0, 1)]

    def deep_xy(s):
        return minus_plus(rows(rxy[s, 0], 4, 7), rows(rxy[s, 1], 3, 0), 1)

    def deep_xz(s):
        return minus_plus(lanes(rxz[s, 0], 61, 127), lanes(rxz[s, 1], 66, 0), 2)

    def near_xy(s):
        return minus_plus(rxy[s, 0], rxy[s, 1], 1)

    def near_xz(s):
        return minus_plus(rxz[s, 0], rxz[s, 1], 2)

    def corner(s):
        line = [[jnp.broadcast_to(rc[s, b, c][None], (1, 8, 128)) for c in (0, 1)] for b in (0, 1)]
        return minus_plus(minus_plus(*line[0], 2), minus_plus(*line[1], 2), 1)

    m10 = join(deep_xy(0), near_xy(0), m10, near_xy(1), deep_xy(1))
    m01 = join(deep_xz(0), near_xz(0), m01, near_xz(1), deep_xz(1))
    m11 = join(
        corner(0), minus_plus(minus_plus(*ryz[0], 2), minus_plus(*ryz[1], 2), 1), corner(1)
    )
    tiles["low"] = grads(m00[0:3], m10[1:2], m01[1:2])
    tiles["high"] = grads(m00[5:8], m10[6:7], m01[6:7])
    tiles["10"] = grads(m10, m00[1:-1], m11)
    tiles["01"] = grads(m01, m11, m00[1:-1])
    tiles["11"] = grads(m11, m01[2:-2], m10[2:-2])

    results = []
    for i in range(26):
        if i in (0, 19):
            results.append(jnp.where(fluid, post[i], pops[i]))
            continue
        c = VEL_ALL[i]
        lo, hi = -c[0], 3 - c[0]
        sx, sy, sz = ((1 - d) // 2 for d in c)

        def from_x():
            k, plane = crossing(0, c[0]).index(i), 5 * sx - 1
            return rx[sx, k : k + 1] + term(i, "high" if sx else "low", plane, plane)

        def t00():
            return along_x(c, post[i], from_x, from_x)

        def t10():
            k = crossing(1, c[1]).index(i)
            packed = rows(y_faces[sy], k + 2, 0) if sy else rows(y_faces[sy], k, 7)

            def edge():
                return rows(rxy[sx, sy], 4, 0) if sy else rows(rxy[sx, sy], 3, 7)

            return along_x(c, packed, edge, edge) + term(i, "10", lo, hi)

        def t01():
            k = crossing(2, c[2]).index(i)
            packed = lanes(rz[sz], k + 2, 0) if sz else lanes(rz[sz], k, 127)

            def edge():
                return lanes(rxz[sx, sz], 64, 0) if sz else lanes(rxz[sx, sz], 63, 127)

            return along_x(c, packed, edge, edge) + term(i, "01", lo, hi)

        def t11():
            packed = rows(ryz[sy][sz], 4, 0) if sy else rows(ryz[sy][sz], 3, 7)
            return packed + term(i, "11", lo, hi)

        came = shift(c, t00, t10, t01, t11)
        back = jnp.where(fluid, post[OPP_ALL[i]], pops[i])
        results.append(jnp.where(flag(i if i < 19 else i - 19), came, back))
    return results


KINDS = {
    "x": (2, 9, 8, 128),
    "y": (2, 5, 8, 128),
    "z": (2, 1, 8, 128),
    "xy": (2, 2, 1, 8, 128),
    "xz": (2, 2, 1, 8, 128),
    "yz": (2, 2, 1, 8, 128),
    "c": (2, 2, 2, 1, 128),
}


def kernel(counts, flow_hbm, phase_hbm, mask_hbm, flow_out, phase_out, *scratch):
    flow_in, phase_in, mask_in, flags, load_sem, send_sem, recv_sem = scratch[:7]
    names = list(KINDS)
    stage_refs = dict(zip(names, scratch[7:14]))
    recv_refs = dict(zip(names, scratch[14:21]))
    loads = [
        pltpu.make_async_copy(src, dst, load_sem.at[n])
        for n, (src, dst) in enumerate(
            ((phase_hbm, phase_in), (mask_hbm, mask_in), (flow_hbm, flow_in))
        )
    ]
    at = [lax.axis_index(a) for a in AXES]

    def exists(o):
        ok = None
        for dim, d in enumerate(o):
            if d:
                here = at[dim] > 0 if d < 0 else at[dim] < counts[dim] - 1
                ok = here if ok is None else jnp.logical_and(ok, here)
        return ok

    def peer(o):
        return tuple(at[dim] + d for dim, d in enumerate(o))

    inside = jnp.logical_and(
        jnp.logical_and(at[0] > 0, at[0] < counts[0] - 1),
        jnp.logical_and(at[2] > 0, at[2] < counts[2] - 1),
    )

    def each(offs, action):
        for dy in (0, -1, 1):
            group = [o for o in offs if o[1] == dy]
            here = inside if dy == 0 else jnp.logical_and(inside, exists((0, dy, 0)))

            @pl.when(here)
            def _(group=group):
                for o in group:
                    action(o)

            @pl.when(jnp.logical_not(inside))
            def _(group=group):
                for o in group:

                    @pl.when(exists(o))
                    def _(o=o):
                        action(o)

    barrier = pltpu.get_barrier_semaphore()

    def greet(o):
        pl.semaphore_signal(barrier, inc=1, device_id=peer(o), device_id_type=MESH)

    for offs in (FAR, ALONG_Z, NEAR):
        each(offs, greet)
    for load in loads:
        load.start()
    for o in OFFS:

        @pl.when(jnp.logical_not(exists(o)))
        def _(o=o):
            for step in range(STEPS):
                ref = part({k: r.at[step] for k, r in recv_refs.items()}, o, True)
                ref[...] = jnp.zeros(ref.shape, jnp.float32)

    near = 1
    for dim in range(3):
        near = near * (
            1
            + (at[dim] > 0).astype(jnp.int32)
            + (at[dim] < counts[dim] - 1).astype(jnp.int32)
        )

    def copy(step, o):
        stage = {k: r.at[step] for k, r in stage_refs.items() if k != "c"}
        recv = {k: r.at[step] for k, r in recv_refs.items()}
        first = step == 0
        if all(o):
            src = stage_refs["c"].at[step, (o[0] + 1) // 2, (o[1] + 1) // 2]
        else:
            src = part(stage, o, first)
        return pltpu.make_async_remote_copy(
            src_ref=src,
            dst_ref=part(recv, neg(o), first),
            send_sem=send_sem.at[step, SLOT[o]],
            recv_sem=recv_sem.at[step, SLOT[neg(o)]],
            device_id=peer(o),
            device_id_type=MESH,
        )

    faces = [o for o in reversed(OFFS) if sum(map(abs, o)) == 1]
    rest = [o for o in reversed(OFFS) if sum(map(abs, o)) > 1]
    for load in loads:
        load.wait()
    fluid = mask_in[...] == 1
    solid = jnp.where(fluid, 1.0, 0.0)
    pops = [flow_in[i] for i in range(19)] + [phase_in[j] for j in range(7)]
    for step in range(STEPS):
        stage = {k: r.at[step] for k, r in stage_refs.items()}
        recv = {k: r.at[step] for k, r in recv_refs.items()}
        local, _, masked = local_part(pops, fluid)
        flag_plane = solid if step == 0 else None

        def wait_recv(o, step=step, recv=recv):
            here = part(recv, o, step == 0)
            pltpu.make_async_remote_copy(
                src_ref=here,
                dst_ref=here,
                send_sem=send_sem.at[step, SLOT[o]],
                recv_sem=recv_sem.at[step, SLOT[o]],
                device_id=peer(o),
                device_id_type=MESH,
            ).wait_recv()

        def send(o, step=step):
            copy(step, o).start()

        groups = ((fill_far, FAR), (fill_along_z, ALONG_Z), (fill_near, NEAR))
        if step == 0:
            for fill, _ in groups:
                fill(stage, local, masked, flag_plane)
            pl.semaphore_wait(barrier, near - 1)
        for fill, offs in groups:
            if step > 0:
                fill(stage, local, masked, flag_plane)
            each(offs, send)
        if step == 1:
            each(OFFS, lambda o: copy(0, o).wait_send())

        def wait_faces(wait_recv=wait_recv):
            each(faces, wait_recv)

        def wait_rest(wait_recv=wait_recv, step=step, recv=recv):
            if step == 1:
                each(OFFS, lambda o: copy(1, o).wait_send())
            each(rest, wait_recv)
            if step == 0:
                for n, value in enumerate(source_flags(recv, solid)):
                    flags[n] = jnp.where(fluid, value, 0.0)
            return lambda i: flags[i - 1] > 0.5

        pops = finish_step(recv, pops, local, masked, fluid, wait_faces, wait_rest)
    for i in range(19):
        flow_out[i] = pops[i]
    for j in range(7):
        phase_out[j] = pops[19 + j]


def drain(flow_in, phase_in, flow_out, phase_out, sems):
    copies = [
        pltpu.make_async_copy(flow_in, flow_out, sems.at[0]),
        pltpu.make_async_copy(phase_in, phase_out, sems.at[1]),
    ]
    for copy in copies:
        copy.start()
    for copy in copies:
        copy.wait()


def solution(mesh):
    counts = [mesh.shape[a] for a in AXES]

    def shards(flow_pops, phase_pops, pore_mask):
        f32 = jnp.float32
        stage_kinds = dict(KINDS, c=(2, 2, 1, 128))
        shapes = (
            jax.ShapeDtypeStruct(flow_pops.shape, f32),
            jax.ShapeDtypeStruct(phase_pops.shape, f32),
        )
        vmem, hbm = pl.BlockSpec(memory_space=pltpu.VMEM), pl.BlockSpec(memory_space=pltpu.HBM)
        results = pl.pallas_call(
            lambda *refs: kernel(counts, *refs),
            out_shape=shapes,
            in_specs=[hbm] * 3,
            out_specs=(vmem, vmem),
            scratch_shapes=[
                pltpu.VMEM((19, 4, 8, 128), f32),
                pltpu.VMEM((7, 4, 8, 128), f32),
                pltpu.VMEM((4, 8, 128), jnp.int32),
                pltpu.VMEM((18, 4, 8, 128), f32),
                pltpu.SemaphoreType.DMA((3,)),
                pltpu.SemaphoreType.DMA((STEPS, 26)),
                pltpu.SemaphoreType.DMA((STEPS, 26)),
            ]
            + [pltpu.VMEM((STEPS, *shape), f32) for shape in stage_kinds.values()]
            + [pltpu.VMEM((STEPS, *shape), f32) for shape in KINDS.values()],
            compiler_params=pltpu.CompilerParams(
                collective_id=0, has_side_effects=True, vmem_limit_bytes=32 << 20
            ),
            name="lattice_steps",
        )(*(pltpu.with_memory_space_constraint(v, pltpu.HBM) for v in (flow_pops, phase_pops, pore_mask)))
        return pl.pallas_call(
            drain,
            out_shape=shapes,
            in_specs=[vmem, vmem],
            out_specs=(hbm, hbm),
            scratch_shapes=[pltpu.SemaphoreType.DMA((2,))],
            name="drain",
        )(*(pltpu.with_memory_space_constraint(v, pltpu.VMEM) for v in results))

    return jax.shard_map(
        shards,
        mesh=mesh,
        in_specs=(P(None, *AXES), P(None, *AXES), P(*AXES)),
        out_specs=(P(None, *AXES), P(None, *AXES)),
        check_vma=False,
    )
```
